128 devices in a mesh: grp: 4 (over y_hi, core), seq: 32 (over y_lo, z, x).
Axes of the slice: x: 4, y: 4 (y_hi: 2, y_lo: 2; y = y_hi * 2 + y_lo), z: 4, core: 2. Of those that a mesh axis runs over, the one named last changes fastest.
Arguments:
- control_x: bfloat16 [10240, 3072], P('seq'), may hold values from -0.29882812 to 0.29882812
- control_qkv: bfloat16 [10240, 3, 1536], P('seq'), may hold values from -40 to 40
- control_out_w: bfloat16 [1536, 3072], replicated, may hold values from -0.15625 to 0.15625
- control_gate: float32 [3072], replicated, may hold values from 1 to 3
- base_x: bfloat16 [10240, 3072], P('seq', 'grp'), may hold values from -0.29882812 to 0.29882812
- base_qkv: bfloat16 [10240, 3, 1536], P('seq', None, 'grp'), may hold values from -40 to 40
- base_out_w: bfloat16 [1536, 3072], P('grp'), may hold values from -0.15625 to 0.15625
- base_gate: float32 [3072], replicated, may hold values from 1 to 3
Outputs:
- control_out: bfloat16 [10240, 3072], P('seq', 'grp')
- base_out: bfloat16 [10240, 3072], P('seq', 'grp')
The draws below stay inside these ranges and needn't reach their ends.
All inputs are finite; a program needn't handle non-finite values.
Results may differ from the reference program's by a relative error of at most 0.017.
Values may be sent and summed in bfloat16 or wider, within the bound.
A program may use at most 512 MiB of HBM per device.

```python
import math
import jax
import jax.numpy as jnp
from jax import lax

D = 3072
HEADS = 12
HD = 128
TOKENS = 10240


def drawn_draw(key):
    columns = HEADS * HD
    third = jax.random.fold_in(key, 2)
    return jnp.clip(jax.random.normal(third, (TOKENS, 3, columns), jnp.float32), -4.0, 4.0)


def draw_control_qkv(key, part):
    key = jax.random.fold_in(key, 11)
    return drawn_draw(key).astype(jnp.bfloat16)


def draw_base_qkv(key, part):
    key = jax.random.fold_in(key, 23)
    return drawn_draw(key).astype(jnp.bfloat16)


def steps_of(own_key, dims, shards, least, high):
    loudness, own = 1.0, jax.random.fold_in(own_key, 6)
    for dim, shards_of in shards:
        heights = jnp.exp(jax.random.uniform(jax.random.fold_in(own, dim), (shards_of,), jnp.float32, least / len(shards), high / len(shards)))
        loudness = loudness * jnp.repeat(heights, dims[dim] // shards_of).reshape([-1 if axis == dim else 1 for axis in range(len(dims))])
    return loudness


def bell_draw(rng, shape, deviation, most, cuts=(), dtype=jnp.bfloat16):
    entries = deviation * jax.random.normal(rng, shape, jnp.float32)
    if cuts:
        entries = entries * steps_of(rng, shape, cuts, -0.22, 0.18)
    return jnp.clip(entries, -most, most).astype(dtype)


def setup_inputs(seed: int = 0) -> dict:
    key_list = jax.random.split(jax.random.key(seed), 9)
    return {
        "control_x": bell_draw(key_list[0], (TOKENS, D), 0.05, 0.29882812, ((0, 32),)),
        "control_qkv": draw_control_qkv(jax.random.fold_in(key_list[8], 71), 0),
        "control_out_w": bell_draw(key_list[2], (HEADS * HD, D), (HEADS * HD) ** -0.5, 0.15625),
        "control_gate": jnp.clip(jax.random.uniform(key_list[3], (D,), jnp.float32, 1.0, 3.0), 1.0, 3.0),
        "base_x": bell_draw(key_list[4], (TOKENS, D), 0.05, 0.29882812, ((0, 32), (1, 4))),
        "base_qkv": draw_base_qkv(jax.random.fold_in(key_list[8], 71), 0),
        "base_out_w": bell_draw(key_list[6], (HEADS * HD, D), (HEADS * HD) ** -0.5, 0.15625, ((0, 4),)),
        "base_gate": jnp.clip(jax.random.uniform(key_list[7], (D,), jnp.float32, 1.0, 3.0), 1.0, 3.0),
    }


def attend(qkv):
    count = qkv.shape[0]
    heads = qkv.shape[2] // HD
    queries = qkv[:, 0].reshape(count, heads, HD).transpose(1, 0, 2)
    keys = qkv[:, 1].reshape(count, heads, HD).transpose(1, 0, 2)
    values = qkv[:, 2].reshape(count, heads, HD).transpose(1, 0, 2)
    factor = 1.0 / math.sqrt(HD)

    def one_head(items):
        query_h, key_h, value_h = items
        scores = jnp.dot(query_h, key_h.T, preferred_element_type=jnp.float32) * factor
        shifted = jnp.exp(scores - lax.optimization_barrier(jnp.max(scores, axis=1, keepdims=True)))
        total = lax.optimization_barrier(jnp.sum(shifted, axis=1))
        summed = jnp.dot(shifted.astype(jnp.bfloat16), value_h, preferred_element_type=jnp.float32)
        return summed / total[:, None]
    result = lax.map(one_head, (queries, keys, values))
    return result.transpose(1, 0, 2).reshape(count, heads * HD).astype(jnp.bfloat16)

def reference(control_x, control_qkv, control_out_w, control_gate, base_x, base_qkv, base_out_w, base_gate):
    control_attention = attend(control_qkv)
    control_proj = jnp.dot(control_attention, control_out_w, preferred_element_type=jnp.float32)
    control_out = (control_x.astype(jnp.float32) + control_gate[None, :] * control_proj).astype(jnp.bfloat16)
    base_attention = attend(base_qkv)
    base_proj = jnp.dot(base_attention, base_out_w, preferred_element_type=jnp.float32)
    base_out = (base_x.astype(jnp.float32) + base_gate[None, :] * base_proj + control_out.astype(jnp.float32)).astype(jnp.bfloat16)
    return (control_out, base_out)
```

```python
import math

import jax
import jax.numpy as jnp
from jax import lax
from jax.experimental import pallas as pl
from jax.experimental.pallas import tpu as pltpu
from jax.sharding import PartitionSpec as P

HD = 128
ROWS = 320
SCALE = 1.4426950408889634 / math.sqrt(HD)
NEG = -1e30
NT = (((1,), (1,)), ((), ()))


def where():
    grp = lax.axis_index("grp")
    seq = lax.axis_index("seq")
    return grp // 2, grp % 2, seq // 16, (seq // 4) % 4, seq % 4


def attend_kernel(
    qkv, control_o, base_o, kv, queries, best, accum, result, q_sem, kv_sem, relay_sem, o_sem, send_sem
):
    half, core, y, z, x = where()
    place = 4 * y + z
    model = x // 2
    here = (half, core, y, z, x)

    def same(a, b):
        hit = a[0] == b[0]
        for left, right in zip(a[1:], b[1:]):
            hit = jnp.logical_and(hit, left == right)
        return hit

    def ident(device):
        return {"grp": 2 * device[0] + device[1], "seq": 16 * device[2] + 4 * device[3] + device[4]}

    barrier = pltpu.get_barrier_semaphore()

    def greet(device):
        pl.semaphore_signal(barrier, inc=1, device_id=ident(device))

    def greet_sources(i, carry):
        greet((half, x % 2, i // 16, (i // 4) % 4, i % 4))
        return carry

    lax.fori_loop(0, 32, greet_sources, 0)

    def greet_control(i, carry):
        chip = (8 * (i % 3) + place) // 3
        greet((i // 6, x // 2, chip // 4, chip % 4, (i // 3) % 2))
        return carry

    lax.fori_loop(0, 12, greet_control, 0)

    def greet_base(i, carry):
        chip = (8 * i + place) // 3
        greet((half, x // 2, chip // 4, chip % 4, 2 + core))
        return carry

    lax.fori_loop(0, 3, greet_base, 0)
    greet((half, 1 - core, y, z, x))
    pl.semaphore_wait(barrier, 33 + jnp.where(model == 0, 24, 6))

    def move(number, source, target, arrived, device, start):
        own = same(device, here)
        remote = pltpu.make_async_remote_copy(
            source, target, send_sem.at[number], arrived, device_id=ident(device)
        )

        @pl.when(jnp.logical_not(own))
        def _():
            if start:
                remote.start()
            else:
                remote.wait_send()

        if start:

            @pl.when(own)
            def _():
                pltpu.make_async_copy(source, target, arrived).start()

    def scatter(start):
        def queries_out(i, carry):
            part, head = i // 3, i % 3
            segment = 8 * head + place
            chip = segment // 3
            move(
                i,
                qkv.at[part, 0, head],
                queries.at[segment % 3, x % 2],
                q_sem.at[0],
                (half, x // 2, chip // 4, chip % 4, 2 * part + core),
                start,
            )
            return carry

        lax.fori_loop(0, 6, queries_out, 0)

        def pairs_out(i, carry):
            part, upper, step = i % 2, (i // 2) % 2, i // 4
            to_y, to_z = (y + upper) % 2, (z + 4 - step) % 4
            chip = 4 * to_y + to_z
            first, last = (3 * chip) // 8, (3 * chip + 2) // 8
            device = (half, y, to_y, to_z, 2 * part + core)
            move(
                6 + i,
                qkv.at[part, pl.ds(1, 2), first],
                kv.at[0, :, z, y, x],
                kv_sem.at[0, z],
                device,
                start,
            )

            @pl.when(last != first)
            def _():
                move(
                    22 + i,
                    qkv.at[part, pl.ds(1, 2), last],
                    kv.at[1, :, z, y, x],
                    kv_sem.at[1, z],
                    device,
                    start,
                )

            return carry

        lax.fori_loop(0, 16, pairs_out, 0)

    scatter(True)

    first, last = (3 * place) // 8, (3 * place + 2) // 8
    for i in range(6):
        best[i] = jnp.full(best.shape[1:], NEG, jnp.float32)
        accum[i] = jnp.zeros(accum.shape[1:], jnp.float32)
    sibling = (half, 1 - core, y, z, x)

    def relay(slot, block):
        return pltpu.make_async_remote_copy(
            kv.at[slot, :, block, core],
            kv.at[slot, :, block, core],
            send_sem.at[38 + 4 * slot + block],
            relay_sem.at[slot, block],
            device_id=ident(sibling),
        )

    def arrive(sem, slot, block, side):
        piece = kv.at[slot, :, block, side]
        pltpu.make_async_copy(piece, piece, sem.at[slot, block]).wait()

    def take_own(block):
        arrive(kv_sem, 0, block, core)
        relay(0, block).start()

        @pl.when(last != first)
        def _():
            arrive(kv_sem, 1, block, core)
            relay(1, block).start()

    def take_sibling(block):
        arrive(relay_sem, 0, block, 1 - core)

        @pl.when(last != first)
        def _():
            arrive(relay_sem, 1, block, 1 - core)

    def update(block, side):
        for i in range(6):
            slot = (3 * place + i // 2) // 8 - first
            keys = kv[slot, 0, block, side].reshape(4 * ROWS, HD)
            values = kv[slot, 1, block, side].reshape(4 * ROWS, HD)
            values = jnp.concatenate([values, jnp.ones_like(values)], axis=1)
            scores = lax.dot_general(
                queries[i // 2, i % 2], keys, NT, preferred_element_type=jnp.float32
            )
            old = best[i][:, :1]
            new = jnp.maximum(old, jnp.max(scores, axis=1, keepdims=True))
            weights = jnp.exp2(scores * SCALE - new * SCALE).astype(jnp.bfloat16)
            keep = jnp.exp2((old - new) * SCALE)
            best[i] = jnp.broadcast_to(new, best.shape[1:])
            accum[i] = accum[i] * keep + jnp.dot(
                weights, values, preferred_element_type=jnp.float32
            )

    whole = queries.at[...]
    pltpu.make_async_copy(whole, whole, q_sem.at[0]).wait()
    take_own(z)

    def step(t, carry):
        block = (z + t) % 4
        update(block, core)

        @pl.when(t < 3)
        def _():
            take_own((block + 1) % 4)

        take_sibling(block)
        update(block, 1 - core)
        return carry

    lax.fori_loop(0, 4, step, 0)

    for i in range(6):
        result[i] = (accum[i][:, :HD] / accum[i][:, HD:]).astype(jnp.bfloat16)

    def home(start):
        for i in range(6):
            segment = 3 * place + i // 2
            head = segment // 8
            token = segment % 8
            owner = (token // 4, token % 4, 2 * core + i % 2)

            @pl.when(model == 0)
            def _():
                column = pl.multiple_of((3 * (2 * half + x) + head) * HD, HD)
                for g in range(4):
                    move(
                        46 + 4 * i + g,
                        result.at[i],
                        control_o.at[:, pl.ds(column, HD)],
                        o_sem.at[0],
                        (g // 2, g % 2) + owner,
                        start,
                    )

            @pl.when(model == 1)
            def _():
                column = pl.multiple_of(head * HD, HD)
                move(
                    70 + i,
                    result.at[i],
                    base_o.at[:, pl.ds(column, HD)],
                    o_sem.at[1],
                    (half, x - 2) + owner,
                    start,
                )

    home(True)
    scatter(False)
    for block in range(4):
        relay(0, block).wait_send()

        @pl.when(last != first)
        def _():
            relay(1, block).wait_send()

    home(False)
    pltpu.make_async_copy(control_o, control_o, o_sem.at[0]).wait()
    pltpu.make_async_copy(base_o, base_o, o_sem.at[1]).wait()


def attend(qkv):
    vmem = pl.BlockSpec(memory_space=pltpu.VMEM)
    return pl.pallas_call(
        attend_kernel,
        out_shape=(
            jax.ShapeDtypeStruct((ROWS, 12 * HD), jnp.bfloat16),
            jax.ShapeDtypeStruct((ROWS, 3 * HD), jnp.bfloat16),
        ),
        in_specs=[vmem],
        out_specs=(vmem, vmem),
        scratch_shapes=[
            pltpu.VMEM((2, 2, 4, 2, 4, ROWS, HD), jnp.bfloat16),
            pltpu.VMEM((3, 2, ROWS, HD), jnp.bfloat16),
            pltpu.VMEM((6, ROWS, HD), jnp.float32),
            pltpu.VMEM((6, ROWS, 2 * HD), jnp.float32),
            pltpu.VMEM((6, ROWS, HD), jnp.bfloat16),
            pltpu.SemaphoreType.DMA((1,)),
            pltpu.SemaphoreType.DMA((2, 4)),
            pltpu.SemaphoreType.DMA((2, 4)),
            pltpu.SemaphoreType.DMA((2,)),
            pltpu.SemaphoreType.DMA((76,)),
        ],
        compiler_params=pltpu.CompilerParams(
            collective_id=0, has_side_effects=True, vmem_limit_bytes=60 * 2**20
        ),
        name="attend",
    )(qkv)


def on_device(
    control_x, control_qkv, control_out_w, control_gate, base_x, base_qkv, base_out_w, base_gate
):
    width = base_x.shape[1]
    group = lax.axis_index("grp")
    columns = base_qkv.shape[2]
    control_part = lax.dynamic_slice_in_dim(control_qkv, group * columns, columns, 2)
    qkv = jnp.stack([control_part, base_qkv]).reshape(2, ROWS, 3, 3, HD).transpose(0, 2, 3, 1, 4)
    control_o, base_o = attend(qkv)
    base_term = jnp.dot(base_o, base_out_w, preferred_element_type=jnp.float32)
    base_proj = lax.psum_scatter(
        base_term.astype(jnp.bfloat16), "grp", scatter_dimension=1, tiled=True
    ).astype(jnp.float32)
    control_w = lax.dynamic_slice_in_dim(control_out_w, group * width, width, 1)
    control_proj = jnp.dot(control_o, control_w, preferred_element_type=jnp.float32)
    control_cols = lax.dynamic_slice_in_dim(control_x, group * width, width, 1)
    control_gain = lax.dynamic_slice_in_dim(control_gate, group * width, width, 0)
    base_gain = lax.dynamic_slice_in_dim(base_gate, group * width, width, 0)
    control_out = (control_cols.astype(jnp.float32) + control_gain[None, :] * control_proj).astype(
        jnp.bfloat16
    )
    base_out = (
        base_x.astype(jnp.float32)
        + base_gain[None, :] * base_proj
        + control_out.astype(jnp.float32)
    ).astype(jnp.bfloat16)
    return (control_out, base_out)


def solution(mesh):
    in_specs = (
        P("seq", None),
        P("seq", None, None),
        P(),
        P(),
        P("seq", "grp"),
        P("seq", None, "grp"),
        P("grp", None),
        P(),
    )
    out_specs = (P("seq", "grp"), P("seq", "grp"))
    return jax.shard_map(
        on_device, mesh=mesh, in_specs=in_specs, out_specs=out_specs, check_vma=False
    )
```

```python
import math

import jax
import jax.numpy as jnp
from jax import lax
from jax.experimental import pallas as pl
from jax.experimental.pallas import tpu as pltpu
from jax.sharding import PartitionSpec as P

HD = 128
ROWS = 320
SCALE = 1.4426950408889634 / math.sqrt(HD)
NEG = -1e30
NT = (((1,), (1,)), ((), ()))


def where():
    grp = lax.axis_index("grp")
    seq = lax.axis_index("seq")
    return grp // 2, grp % 2, seq // 16, (seq // 4) % 4, seq % 4


def attend_kernel(
    control,
    base,
    control_o,
    base_o,
    kv,
    queries,
    best,
    accum,
    part_out,
    part_in,
    result,
    x_sem,
    q_sem,
    z_sem,
    far_sem,
    relay_sem,
    part_sem,
    o_sem,
    send_sem,
):
    half, core, y, z, x = where()
    model = x // 2
    here = (half, core, y, z, x)
    sibling = (half, 1 - core, y, z, x)
    above = (half, core, y, (z + 1) % 4, x)
    below = (half, core, y, (z + 3) % 4, x)
    across = (half, core, 1 - y, z, x)

    def same(a, b):
        hit = a[0] == b[0]
        for left, right in zip(a[1:], b[1:]):
            hit = jnp.logical_and(hit, left == right)
        return hit

    def ident(device):
        return {"grp": 2 * device[0] + device[1], "seq": 16 * device[2] + 4 * device[3] + device[4]}

    barrier = pltpu.get_barrier_semaphore()
    for device in (
        [sibling, above, below, across]
        + [(half, x % 2, y, z, 2 * core + i) for i in range(2)]
        + [(half, x // 2, y, z, 2 + core)]
        + [(i, x // 2, y, z, core) for i in range(2)]
    ):
        pl.semaphore_signal(barrier, inc=1, device_id=ident(device))
    pl.semaphore_wait(barrier, 6 + jnp.where(model == 0, 4, 2))

    sends = []

    def send(source, target, arrived, device, may_be_here=False, when=None):
        remote = pltpu.make_async_remote_copy(
            source, target, send_sem.at[len(sends)], arrived, device_id=ident(device)
        )
        away = None
        if may_be_here:
            own = same(device, here)
            away = jnp.logical_not(own)
            if when is not None:
                own, away = jnp.logical_and(own, when), jnp.logical_and(away, when)

            @pl.when(own)
            def _():
                pltpu.make_async_copy(source, target, arrived).start()

            pl.when(away)(remote.start)
        else:
            away = when
            if when is None:
                remote.start()
            else:
                pl.when(when)(remote.start)
        sends.append((remote, away))

    def finish_sends():
        for remote, away in sends:
            if away is None:
                remote.wait_send()
            else:
                pl.when(away)(remote.wait_send)

    def arrive(ref, sem):
        pltpu.make_async_copy(ref, ref, sem).wait()

    group = 2 * half + core
    columns = pl.ds(pl.multiple_of(group * 3 * HD, 3 * HD), 3 * HD)
    for part, ref in ((0, control.at[:, :, columns]), (1, base)):
        target = (half, x // 2, y, z, 2 * part + core)
        send(ref.at[pl.ds(1, 2)], kv.at[0, 0, x % 2], x_sem.at[x % 2], target, True)
    for part, ref in ((0, control.at[:, :, columns]), (1, base)):
        target = (half, x // 2, y, z, 2 * part + core)
        send(ref.at[0], queries.at[0, x % 2], q_sem.at[0, x % 2], target, True)

    best[...] = jnp.full(best.shape, NEG, jnp.float32)
    accum[...] = jnp.zeros(accum.shape, jnp.float32)

    near = jnp.where(x // 2 == core, x % 2, 1 - x % 2)

    for i in (near, 1 - near):
        arrive(kv.at[0, 0, i], x_sem.at[i])
        send(kv.at[0, 0, i], kv.at[1, 0, i], z_sem.at[0, i], above)
        send(kv.at[0, 0, i], kv.at[2, 0, i], z_sem.at[1, i], below)
        send(kv.at[0, 0, i], kv.at[0, 1, i], relay_sem.at[0, i], sibling)
    for i in (near, 1 - near):
        arrive(queries.at[0, i], q_sem.at[0, i])
        send(queries.at[0, i], queries.at[1, i], q_sem.at[1, i], across)

    def neighbours(i):
        arrive(kv.at[1, 0, i], z_sem.at[0, i])
        send(kv.at[1, 0, i, 0], kv.at[3, 0, i, 0], far_sem.at[0, i], above)
        send(kv.at[1, 0, i], kv.at[1, 1, i], relay_sem.at[1, i], sibling)
        arrive(kv.at[2, 0, i], z_sem.at[1, i])
        send(kv.at[2, 0, i, 1], kv.at[3, 0, i, 1], far_sem.at[1, i], below)
        send(kv.at[2, 0, i], kv.at[2, 1, i], relay_sem.at[2, i], sibling)

    def far(i):
        for j in range(2):
            arrive(kv.at[3, 0, i, j], far_sem.at[j, i])
        send(kv.at[3, 0, i], kv.at[3, 1, i], relay_sem.at[3, i], sibling)

    def relayed(block):
        for i in range(2):
            arrive(kv.at[block, 1, i], relay_sem.at[block, i])

    def update(block, side):
        for head in range(3):
            lanes = pl.ds(head * HD, HD)
            keys = kv[block, :, :, 0, :, lanes].reshape(4 * ROWS, HD)
            values = kv[block, :, :, 1, :, lanes].reshape(4 * ROWS, HD)
            values = jnp.concatenate([values, jnp.ones_like(values)], axis=1)
            for i in range(2):
                scores = lax.dot_general(
                    queries[side, i, :, lanes], keys, NT, preferred_element_type=jnp.float32
                )
                old = best[side, i, head][:, :1]
                new = jnp.maximum(old, jnp.max(scores, axis=1, keepdims=True))
                weights = jnp.exp2(scores * SCALE - new * SCALE).astype(jnp.bfloat16)
                keep = jnp.exp2((old - new) * SCALE)
                best[side, i, head] = jnp.broadcast_to(new, best.shape[3:])
                accum[side, i, head] = accum[side, i, head] * keep + jnp.dot(
                    weights, values, preferred_element_type=jnp.float32
                )

    def both(block):
        def one(side, carry):
            update(block, side)
            return carry

        lax.fori_loop(0, 2, one, 0)

    def outcome(side, i, head):
        total = accum[side, i, head][:, HD:]
        log_sum = best[side, i, head] * SCALE + jnp.log2(total)
        return accum[side, i, head][:, :HD] / total, log_sum

    relayed(0)
    update(0, 0)
    neighbours(0)
    for i in range(2):
        arrive(queries.at[1, i], q_sem.at[1, i])
    update(0, 1)
    neighbours(1)
    relayed(1)
    both(1)
    far(0)
    relayed(2)
    both(2)
    far(1)
    relayed(3)
    update(3, 1)

    lane = lax.broadcasted_iota(jnp.int32, (ROWS, HD), 1)
    for i in range(2):
        packed = jnp.zeros((ROWS, HD), jnp.float32)
        for head in range(3):
            value, rest = outcome(1, i, head)
            part_out[i, :, head * HD : (head + 1) * HD] = value.astype(jnp.bfloat16)
            for j in range(3):
                piece = rest.astype(jnp.bfloat16).astype(jnp.float32)
                packed = jnp.where(lane == 3 * head + j, piece, packed)
                rest = rest - piece
        part_out[i, :, 3 * HD :] = packed.astype(jnp.bfloat16)
        send(part_out.at[i], part_in.at[i], part_sem.at[i], across)
    update(3, 0)

    home_columns = pl.ds(pl.multiple_of((2 * half + x % 2) * 3 * HD, 3 * HD), 3 * HD)
    for i in range(2):
        arrive(part_in.at[i], part_sem.at[i])
        packed = part_in[i, :, 3 * HD :].astype(jnp.float32)
        for head in range(3):
            value, log_sum = outcome(0, i, head)
            other = (
                packed[:, 3 * head : 3 * head + 1]
                + packed[:, 3 * head + 1 : 3 * head + 2]
                + packed[:, 3 * head + 2 : 3 * head + 3]
            )
            top = jnp.maximum(log_sum, other)
            mine = jnp.exp2(log_sum - top)
            theirs = jnp.exp2(other - top)
            theirs_value = part_in[i, :, head * HD : (head + 1) * HD].astype(jnp.float32)
            mixed = (value * mine + theirs_value * theirs) / (mine + theirs)
            result[i, :, head * HD : (head + 1) * HD] = mixed.astype(jnp.bfloat16)
        for g in range(2):
            owner = (g, x % 2, y, z, 2 * core + i)
            target = control_o.at[:, home_columns]
            send(result.at[i], target, o_sem.at[half], owner, True, model == 0)
        owner = (half, x % 2, y, z, 2 * core + i)
        send(result.at[i], base_o, o_sem.at[2], owner, True, model == 1)

    for g in range(2):
        source = control_o.at[:, pl.ds(pl.multiple_of((2 * g + core) * 3 * HD, 3 * HD), 3 * HD)]
        arrive(source, o_sem.at[g])
        send(source, source, o_sem.at[3 + g], sibling)
    for g in range(2):
        target = control_o.at[
            :, pl.ds(pl.multiple_of((2 * g + 1 - core) * 3 * HD, 3 * HD), 3 * HD)
        ]
        arrive(target, o_sem.at[3 + g])
    arrive(base_o, o_sem.at[2])
    finish_sends()


def attend(control, base):
    vmem = pl.BlockSpec(memory_space=pltpu.VMEM)
    anywhere = pl.BlockSpec(memory_space=pl.ANY)
    dma = pltpu.SemaphoreType.DMA
    return pl.pallas_call(
        attend_kernel,
        out_shape=(
            jax.ShapeDtypeStruct((ROWS, 12 * HD), jnp.bfloat16),
            jax.ShapeDtypeStruct((ROWS, 3 * HD), jnp.bfloat16),
        ),
        in_specs=[anywhere, anywhere],
        out_specs=(vmem, vmem),
        scratch_shapes=[
            pltpu.VMEM((4, 2, 2, 2, ROWS, 3 * HD), jnp.bfloat16),
            pltpu.VMEM((2, 2, ROWS, 3 * HD), jnp.bfloat16),
            pltpu.VMEM((2, 2, 3, ROWS, HD), jnp.float32),
            pltpu.VMEM((2, 2, 3, ROWS, 2 * HD), jnp.float32),
            pltpu.VMEM((2, ROWS, 4 * HD), jnp.bfloat16),
            pltpu.VMEM((2, ROWS, 4 * HD), jnp.bfloat16),
            pltpu.VMEM((2, ROWS, 3 * HD), jnp.bfloat16),
            dma((2,)),
            dma((2, 2)),
            dma((2, 2)),
            dma((2, 2)),
            dma((4, 2)),
            dma((2,)),
            dma((5,)),
            dma((40,)),
        ],
        compiler_params=pltpu.CompilerParams(
            collective_id=0, has_side_effects=True, vmem_limit_bytes=60 * 2**20
        ),
        name="attend",
    )(control, base)


def on_device(
    control_x, control_qkv, control_out_w, control_gate, base_x, base_qkv, base_out_w, base_gate
):
    width = base_x.shape[1]
    group = lax.axis_index("grp")
    control_o, base_o = attend(control_qkv.transpose(1, 0, 2), base_qkv.transpose(1, 0, 2))
    base_term = jnp.dot(base_o, base_out_w, preferred_element_type=jnp.float32)
    base_proj = lax.psum_scatter(
        base_term.astype(jnp.bfloat16), "grp", scatter_dimension=1, tiled=True
    ).astype(jnp.float32)
    control_w = lax.dynamic_slice_in_dim(control_out_w, group * width, width, 1)
    control_proj = jnp.dot(control_o, control_w, preferred_element_type=jnp.float32)
    control_cols = lax.dynamic_slice_in_dim(control_x, group * width, width, 1)
    control_gain = lax.dynamic_slice_in_dim(control_gate, group * width, width, 0)
    base_gain = lax.dynamic_slice_in_dim(base_gate, group * width, width, 0)
    control_out = (control_cols.astype(jnp.float32) + control_gain[None, :] * control_proj).astype(
        jnp.bfloat16
    )
    base_out = (
        base_x.astype(jnp.float32)
        + base_gain[None, :] * base_proj
        + control_out.astype(jnp.float32)
    ).astype(jnp.bfloat16)
    return (control_out, base_out)


def solution(mesh):
    in_specs = (
        P("seq", None),
        P("seq", None, None),
        P(),
        P(),
        P("seq", "grp"),
        P("seq", None, "grp"),
        P("grp", None),
        P(),
    )
    out_specs = (P("seq", "grp"), P("seq", "grp"))
    return jax.shard_map(
        on_device, mesh=mesh, in_specs=in_specs, out_specs=out_specs, check_vma=False
    )
```

```python
import math

import jax
import jax.numpy as jnp
from jax import lax
from jax.experimental import pallas as pl
from jax.experimental.pallas import tpu as pltpu
from jax.sharding import PartitionSpec as P

HD = 128
ROWS = 320
WIDTH = 768
GROUP = 3 * HD
SHARE = GROUP // 4
SCALE = 1.4426950408889634 / math.sqrt(HD)
NEG = -1e30
NT = (((1,), (1,)), ((), ()))
PER_HEAD = 31


def sublayer_kernel(
    control_x,
    control,
    control_w,
    control_gate,
    base_x,
    base,
    base_w,
    base_gate,
    control_out,
    base_out,
    kv,
    queries,
    best,
    accum,
    own_value,
    own_sum,
    part_out,
    part_in,
    result,
    merged,
    w_control,
    w_base,
    proj,
    x_control,
    x_base,
    x_sem,
    q_sem,
    z_sem,
    far_sem,
    relay_sem,
    part_sem,
    o_sem,
    hand_sem,
    w_sem,
    local_sem,
    send_sem,
):
    grp = lax.axis_index("grp")
    seq = lax.axis_index("seq")
    half, core, y, z, x = grp // 2, grp % 2, seq // 16, (seq // 4) % 4, seq % 4
    model = x // 2
    here = (half, core, y, z, x)
    sibling = (half, 1 - core, y, z, x)
    above = (half, core, y, (z + 1) % 4, x)
    below = (half, core, y, (z + 3) % 4, x)
    across = (half, core, 1 - y, z, x)

    def ident(device):
        return {"grp": 2 * device[0] + device[1], "seq": 16 * device[2] + 4 * device[3] + device[4]}

    barrier = pltpu.get_barrier_semaphore()
    greeted = (
        [sibling, above, below, across]
        + [(half, x % 2, y, z, 2 * core + i) for i in range(2)]
        + [(f, x // 2, y, z, 2 * m + core) for f in range(2) for m in range(2)]
        + [(1 - half, i, y, z, x) for i in range(2)]
        + [(half, core, y, z, (x + d) % 4) for d in range(1, 4)]
    )
    for device in greeted:
        pl.semaphore_signal(barrier, inc=1, device_id=ident(device))

    lanes_out = pl.ds(pl.multiple_of(grp * WIDTH, WIDTH), WIDTH)
    locals_in = [
        pltpu.make_async_copy(control_w.at[:, :, lanes_out], w_control, local_sem.at[0]),
        pltpu.make_async_copy(base_w.at[:, lanes_out], w_base.at[grp], local_sem.at[1]),
        pltpu.make_async_copy(control_x.at[:, lanes_out], x_control, local_sem.at[2]),
        pltpu.make_async_copy(base_x, x_base, local_sem.at[3]),
    ]

    pl.semaphore_wait(barrier, len(greeted))

    def send(number, source, target, arrived, device, start, may_be_here=False):
        remote = pltpu.make_async_remote_copy(
            source, target, send_sem.at[number], arrived, device_id=ident(device)
        )
        act = remote.start if start else remote.wait_send
        if not may_be_here:
            act()
            return
        own = device[0] == here[0]
        for left, right in zip(device[1:], here[1:]):
            own = jnp.logical_and(own, left == right)
        pl.when(jnp.logical_not(own))(act)
        if start:

            @pl.when(own)
            def _():
                pltpu.make_async_copy(source, target, arrived).start()

    def arrive(ref, sem):
        pltpu.make_async_copy(ref, ref, sem).wait()

    def lanes(index):
        return pl.ds(pl.multiple_of(index * HD, HD), HD)

    def pairs_out(h, start):
        for m, ref, index in ((0, control, 3 * grp + h), (1, base, h)):
            send(
                PER_HEAD * h + m,
                ref.at[pl.ds(1, 2), :, lanes(index)],
                kv.at[h, :, 0, 0, x % 2],
                x_sem.at[h, x % 2],
                (half, x // 2, y, z, 2 * m + core),
                start,
                True,
            )

    def queries_out(h, start):
        for m, ref, index in ((0, control, 3 * grp + h), (1, base, h)):
            send(
                PER_HEAD * h + 2 + m,
                ref.at[0, :, lanes(index)],
                queries.at[h, 0, x % 2],
                q_sem.at[h, 0, x % 2],
                (half, x // 2, y, z, 2 * m + core),
                start,
                True,
            )

    def ring_out(h, i, start):
        block = kv.at[h, :, 0, 0, i]
        number = PER_HEAD * h + i
        send(number + 4, block, kv.at[h, :, 1, 0, i], z_sem.at[h, 0, i], above, start)
        send(number + 6, block, kv.at[h, :, 2, 0, i], z_sem.at[h, 1, i], below, start)
        send(number + 8, block, kv.at[h, :, 0, 1, i], relay_sem.at[h, 0, i], sibling, start)

    def query_across(h, i, start):
        send(
            PER_HEAD * h + 10 + i,
            queries.at[h, 0, i],
            queries.at[h, 1, i],
            q_sem.at[h, 1, i],
            across,
            start,
        )

    def keys_on(h, i, start):
        number = PER_HEAD * h + i
        send(number + 12, kv.at[h, 0, 1, 0, i], kv.at[h, 0, 3, 0, i], far_sem.at[h, 0, i], above, start)
        block = kv.at[h, :, 1, 0, i]
        send(number + 16, block, kv.at[h, :, 1, 1, i], relay_sem.at[h, 1, i], sibling, start)

    def values_on(h, i, start):
        number = PER_HEAD * h + i
        send(number + 14, kv.at[h, 1, 2, 0, i], kv.at[h, 1, 3, 0, i], far_sem.at[h, 1, i], below, start)
        block = kv.at[h, :, 2, 0, i]
        send(number + 18, block, kv.at[h, :, 2, 1, i], relay_sem.at[h, 2, i], sibling, start)

    def far_on(h, i, start):
        block = kv.at[h, :, 3, 0, i]
        send(PER_HEAD * h + 20 + i, block, kv.at[h, :, 3, 1, i], relay_sem.at[h, 3, i], sibling, start)

    def part_across(h, start):
        send(PER_HEAD * h + 22, part_out.at[h], part_in.at[h], part_sem.at[h], across, start)

    def home(h, start):
        for i in range(2):
            for f in range(2):
                send(
                    PER_HEAD * h + 23 + 2 * i + f,
                    result.at[h, i],
                    merged.at[h, model, :, lanes(2 * half + x % 2)],
                    o_sem.at[h, model, half],
                    (f, x % 2, y, z, 2 * core + i),
                    start,
                    True,
                )

    def hand_over(h, m, f, start):
        block = merged.at[h, m, :, lanes(2 * f + core)]
        send(PER_HEAD * h + 27 + 2 * m + f, block, block, hand_sem.at[h, m, f], sibling, start)

    last = 3 * PER_HEAD
    share = pl.ds(pl.multiple_of(SHARE * x, SHARE), SHARE)

    def weights_beside(start):
        columns = pl.ds(pl.multiple_of((2 * half + 1 - core) * WIDTH, WIDTH), WIDTH)
        send(last, base_w.at[:, columns], w_base.at[grp], w_sem.at[0], sibling, start)

    def weights_across(start):
        for c in range(2):
            columns = pl.ds(pl.multiple_of((2 * (1 - half) + c) * WIDTH, WIDTH), WIDTH)
            send(
                last + 1 + c,
                base_w.at[share, columns],
                w_base.at[grp, share],
                w_sem.at[1 + core],
                (1 - half, c, y, z, x),
                start,
            )

    def weights_along(start):
        for d in range(1, 4):
            block = w_base.at[pl.ds(2 * (1 - half), 2), share]
            send(
                last + 2 + d, block, block, w_sem.at[2 + d], (half, core, y, z, (x + d) % 4), start
            )

    near = jnp.where(x // 2 == core, x % 2, 1 - x % 2)

    def blocks_in(h):
        for i in (near, 1 - near):
            arrive(kv.at[h, :, 0, 0, i], x_sem.at[h, i])
            ring_out(h, i, True)
        for i in (near, 1 - near):
            arrive(queries.at[h, 0, i], q_sem.at[h, 0, i])
            query_across(h, i, True)

    def neighbours_in(h):
        for i in (near, 1 - near):
            arrive(kv.at[h, :, 1, 0, i], z_sem.at[h, 0, i])
            keys_on(h, i, True)
            arrive(kv.at[h, :, 2, 0, i], z_sem.at[h, 1, i])
            values_on(h, i, True)

    def far_in(h):
        for i in (near, 1 - near):
            for j in range(2):
                arrive(kv.at[h, j, 3, 0, i], far_sem.at[h, j, i])
            far_on(h, i, True)

    def relayed(h, block):
        for i in range(2):
            arrive(kv.at[h, :, block, 1, i], relay_sem.at[h, block, i])

    def update(h, low, count):
        keys = kv[h, 0, low : low + count].reshape(count * 4 * ROWS, HD)
        values = kv[h, 1, low : low + count].reshape(count * 4 * ROWS, HD)
        values = jnp.concatenate([values, jnp.ones_like(values)], axis=1)
        for side in range(2):
            for i in range(2):
                scores = lax.dot_general(
                    queries[h, side, i], keys, NT, preferred_element_type=jnp.float32
                )
                old = best[side, i][:, :1]
                new = jnp.maximum(old, jnp.max(scores, axis=1, keepdims=True))
                weights = jnp.exp2(scores * SCALE - new * SCALE).astype(jnp.bfloat16)
                keep = jnp.exp2((old - new) * SCALE)
                best[side, i] = jnp.broadcast_to(new, best.shape[2:])
                accum[side, i] = accum[side, i] * keep + jnp.dot(
                    weights, values, preferred_element_type=jnp.float32
                )

    lane = lax.broadcasted_iota(jnp.int32, (ROWS, HD), 1)

    def outcome(side, i):
        total = accum[side, i][:, HD:]
        return accum[side, i][:, :HD] / total, best[side, i] * SCALE + jnp.log2(total)

    def part(h):
        packed = jnp.zeros((ROWS, HD), jnp.float32)
        for i in range(2):
            value, rest = outcome(1, i)
            part_out[h, i] = value.astype(jnp.bfloat16)
            for j in range(3):
                piece = rest.astype(jnp.bfloat16).astype(jnp.float32)
                packed = jnp.where(lane == 3 * i + j, piece, packed)
                rest = rest - piece
        part_out[h, 2] = packed.astype(jnp.bfloat16)
        part_across(h, True)
        for i in range(2):
            own_value[i], own_sum[i] = outcome(0, i)

    def combine(h):
        arrive(part_in.at[h], part_sem.at[h])
        packed = part_in[h, 2].astype(jnp.float32)
        for i in range(2):
            other = (
                packed[:, 3 * i : 3 * i + 1]
                + packed[:, 3 * i + 1 : 3 * i + 2]
                + packed[:, 3 * i + 2 : 3 * i + 3]
            )
            top = jnp.maximum(own_sum[i], other)
            mine = jnp.exp2(own_sum[i] - top)
            theirs = jnp.exp2(other - top)
            mixed = own_value[i] * mine + part_in[h, i].astype(jnp.float32) * theirs
            result[h, i] = (mixed / (mine + theirs)).astype(jnp.bfloat16)
        home(h, True)

    def results_in(h):
        for m in range(2):
            for f in range(2):
                arrive(merged.at[h, m, :, lanes(2 * f + core)], o_sem.at[h, m, f])
                hand_over(h, m, f, True)

    def project(h):
        for m in range(2):
            for f in range(2):
                arrive(merged.at[h, m, :, lanes(2 * f + 1 - core)], hand_sem.at[h, m, f])
        for m, weight in ((0, w_control), (1, w_base)):
            rows = weight[:, h * HD : (h + 1) * HD].reshape(4 * HD, WIDTH)
            term = jnp.dot(merged[h, m], rows, preferred_element_type=jnp.float32)
            proj[m] = term if h == 0 else proj[m] + term

    for h in range(3):
        pairs_out(h, True)
        queries_out(h, True)
    weights_beside(True)
    for copy in locals_in:
        copy.start()
    blocks_in(0)

    def head_step(h, carry):
        best[...] = jnp.full(best.shape, NEG, jnp.float32)
        accum[...] = jnp.zeros(accum.shape, jnp.float32)
        relayed(h, 0)
        for i in range(2):
            arrive(queries.at[h, 1, i], q_sem.at[h, 1, i])
        update(h, 0, 1)

        @pl.when(h < 2)
        def _():
            blocks_in(h + 1)

        neighbours_in(h)

        @pl.when(h == 0)
        def _():
            weights_across(True)

        @pl.when(h == 1)
        def _():
            for c in range(2):
                arrive(w_base.at[2 * (1 - half) + c, share], w_sem.at[1 + c])
            weights_along(True)

        @pl.when(h > 0)
        def _():
            combine(h - 1)

        relayed(h, 1)
        relayed(h, 2)
        update(h, 1, 2)
        far_in(h)
        relayed(h, 3)
        update(h, 3, 1)
        part(h)
        return carry

    lax.fori_loop(0, 3, head_step, 0)

    results_in(0)
    for copy in locals_in:
        copy.wait()
    arrive(w_base.at[2 * half + 1 - core], w_sem.at[0])
    for d in range(1, 4):
        rows = pl.ds(pl.multiple_of(SHARE * ((x + 4 - d) % 4), SHARE), SHARE)
        arrive(w_base.at[pl.ds(2 * (1 - half), 2), rows], w_sem.at[2 + d])
    project(0)
    results_in(1)
    combine(2)
    project(1)
    results_in(2)
    project(2)

    for k in range(WIDTH // HD):
        part_lanes = slice(k * HD, (k + 1) * HD)
        row = pl.ds(grp * (WIDTH // HD) + k, 1)
        first = x_control[:, part_lanes].astype(jnp.float32) + control_gate[row, :] * proj[0, :, part_lanes]
        first = first.astype(jnp.bfloat16)
        control_out[:, part_lanes] = first
        second = x_base[:, part_lanes].astype(jnp.float32) + base_gate[row, :] * proj[1, :, part_lanes]
        base_out[:, part_lanes] = (second + first.astype(jnp.float32)).astype(jnp.bfloat16)

    def finish(h, carry):
        pairs_out(h, False)
        queries_out(h, False)
        for i in range(2):
            ring_out(h, i, False)
            query_across(h, i, False)
            keys_on(h, i, False)
            values_on(h, i, False)
            far_on(h, i, False)
        part_across(h, False)
        home(h, False)
        for m in range(2):
            for f in range(2):
                hand_over(h, m, f, False)
        return carry

    lax.fori_loop(0, 3, finish, 0)
    weights_beside(False)
    weights_across(False)
    weights_along(False)


def on_device(
    control_x, control_qkv, control_out_w, control_gate, base_x, base_qkv, base_out_w, base_gate
):
    vmem = pl.BlockSpec(memory_space=pltpu.VMEM)
    anywhere = pl.BlockSpec(memory_space=pl.ANY)
    dma = pltpu.SemaphoreType.DMA
    half16 = jnp.bfloat16
    full32 = jnp.float32
    shape = jax.ShapeDtypeStruct((ROWS, WIDTH), half16)
    return pl.pallas_call(
        sublayer_kernel,
        out_shape=(shape, shape),
        in_specs=[anywhere, anywhere, anywhere, vmem, anywhere, anywhere, anywhere, vmem],
        out_specs=(vmem, vmem),
        scratch_shapes=[
            pltpu.VMEM((3, 2, 4, 2, 2, ROWS, HD), half16),
            pltpu.VMEM((3, 2, 2, ROWS, HD), half16),
            pltpu.VMEM((2, 2, ROWS, HD), full32),
            pltpu.VMEM((2, 2, ROWS, 2 * HD), full32),
            pltpu.VMEM((2, ROWS, HD), full32),
            pltpu.VMEM((2, ROWS, HD), full32),
            pltpu.VMEM((3, 3, ROWS, HD), half16),
            pltpu.VMEM((3, 3, ROWS, HD), half16),
            pltpu.VMEM((3, 2, ROWS, HD), half16),
            pltpu.VMEM((3, 2, ROWS, 4 * HD), half16),
            pltpu.VMEM((4, GROUP, WIDTH), half16),
            pltpu.VMEM((4, GROUP, WIDTH), half16),
            pltpu.VMEM((2, ROWS, WIDTH), full32),
            pltpu.VMEM((ROWS, WIDTH), half16),
            pltpu.VMEM((ROWS, WIDTH), half16),
            dma((3, 2)),
            dma((3, 2, 2)),
            dma((3, 2, 2)),
            dma((3, 2, 2)),
            dma((3, 4, 2)),
            dma((3,)),
            dma((3, 2, 2)),
            dma((3, 2, 2)),
            dma((6,)),
            dma((4,)),
            dma((3 * PER_HEAD + 6,)),
        ],
        compiler_params=pltpu.CompilerParams(
            collective_id=0, has_side_effects=True, vmem_limit_bytes=60 * 2**20
        ),
        name="sublayer",
    )(
        control_x,
        control_qkv.transpose(1, 0, 2),
        control_out_w.reshape(4, GROUP, 4 * WIDTH),
        control_gate.reshape(4 * WIDTH // HD, HD),
        base_x,
        base_qkv.transpose(1, 0, 2),
        base_out_w,
        base_gate.reshape(4 * WIDTH // HD, HD),
    )


def solution(mesh):
    in_specs = (
        P("seq", None),
        P("seq", None, None),
        P(),
        P(),
        P("seq", "grp"),
        P("seq", None, "grp"),
        P("grp", None),
        P(),
    )
    out_specs = (P("seq", "grp"), P("seq", "grp"))
    return jax.shard_map(
        on_device, mesh=mesh, in_specs=in_specs, out_specs=out_specs, check_vma=False
    )
```

```python
import math

import jax
import jax.numpy as jnp
from jax import lax
from jax.experimental import pallas as pl
from jax.experimental.pallas import tpu as pltpu
from jax.sharding import PartitionSpec as P

HD = 128
ROWS = 320
WIDTH = 768
GROUP = 3 * HD
SHARE = GROUP // 4
SCALE = 1.4426950408889634 / math.sqrt(HD)
NEG = -1e30
NT = (((1,), (1,)), ((), ()))
PER_HEAD = 31


def sublayer_kernel(
    control_x,
    control,
    control_w,
    control_gate,
    base_x,
    base,
    base_w,
    base_gate,
    control_out,
    base_out,
    kv,
    queries,
    best,
    accum,
    part_out,
    part_in,
    result,
    merged,
    w_control,
    w_base,
    proj,
    x_control,
    x_base,
    x_sem,
    q_sem,
    z_sem,
    far_sem,
    relay_sem,
    part_sem,
    o_sem,
    hand_sem,
    w_sem,
    local_sem,
    send_sem,
):
    grp = lax.axis_index("grp")
    seq = lax.axis_index("seq")
    half, core, y, z, x = grp // 2, grp % 2, seq // 16, (seq // 4) % 4, seq % 4
    model = x // 2
    here = (half, core, y, z, x)
    sibling = (half, 1 - core, y, z, x)
    above = (half, core, y, (z + 1) % 4, x)
    below = (half, core, y, (z + 3) % 4, x)
    across = (half, core, 1 - y, z, x)

    def ident(device):
        return {"grp": 2 * device[0] + device[1], "seq": 16 * device[2] + 4 * device[3] + device[4]}

    barrier = pltpu.get_barrier_semaphore()
    greeted = (
        [sibling, above, below, across]
        + [(half, x % 2, p, z, 2 * core + i) for i in range(2) for p in (y, 1 - y)]
        + [(f, x // 2, p, z, 2 * m + core) for f in range(2) for m in range(2) for p in (y, 1 - y)]
        + [(1 - half, i, y, z, x) for i in range(2)]
        + [(half, core, y, z, (x + d) % 4) for d in range(1, 4)]
    )
    for device in greeted:
        pl.semaphore_signal(barrier, inc=1, device_id=ident(device))

    lanes_out = pl.ds(pl.multiple_of(grp * WIDTH, WIDTH), WIDTH)
    locals_in = [
        pltpu.make_async_copy(control_w.at[:, :, lanes_out], w_control, local_sem.at[0]),
        pltpu.make_async_copy(base_w.at[:, lanes_out], w_base.at[grp], local_sem.at[1]),
        pltpu.make_async_copy(control_x.at[:, lanes_out], x_control, local_sem.at[2]),
        pltpu.make_async_copy(base_x, x_base, local_sem.at[3]),
    ]

    pl.semaphore_wait(barrier, len(greeted))

    def send(number, source, target, arrived, device, start, may_be_here=False):
        remote = pltpu.make_async_remote_copy(
            source, target, send_sem.at[number], arrived, device_id=ident(device)
        )
        act = remote.start if start else remote.wait_send
        if not may_be_here:
            act()
            return
        own = device[0] == here[0]
        for left, right in zip(device[1:], here[1:]):
            own = jnp.logical_and(own, left == right)
        pl.when(jnp.logical_not(own))(act)
        if start:

            @pl.when(own)
            def _():
                pltpu.make_async_copy(source, target, arrived).start()

    def arrive(ref, sem):
        pltpu.make_async_copy(ref, ref, sem).wait()

    def lanes(index):
        return pl.ds(pl.multiple_of(index * HD, HD), HD)

    def route(slot):
        if slot == 1:
            return 1, y
        plane = y if slot == 0 else 1 - y
        return 2 * plane, plane

    def pairs_out(slot, start):
        head, plane = route(slot)
        for m, ref, index in ((0, control, 3 * grp + head), (1, base, head)):
            send(
                PER_HEAD * slot + m,
                ref.at[pl.ds(1, 2), :, lanes(index)],
                kv.at[slot, :, 0, 0, x % 2],
                x_sem.at[slot, x % 2],
                (half, x // 2, plane, z, 2 * m + core),
                start,
                True,
            )

    def queries_out(slot, start):
        head, plane = route(slot)
        for m, ref, index in ((0, control, 3 * grp + head), (1, base, head)):
            send(
                PER_HEAD * slot + 2 + m,
                ref.at[0, :, lanes(index)],
                queries.at[slot % 2, slot // 2, x % 2],
                q_sem.at[slot % 2, slot // 2, x % 2],
                (half, x // 2, plane, z, 2 * m + core),
                start,
                True,
            )

    def ring_out(h, i, start):
        block = kv.at[h, :, 0, 0, i]
        number = PER_HEAD * h + i
        send(number + 4, block, kv.at[h, :, 1, 0, i], z_sem.at[h, 0, i], above, start)
        send(number + 6, block, kv.at[h, :, 2, 0, i], z_sem.at[h, 1, i], below, start)
        send(number + 8, block, kv.at[h, :, 0, 1, i], relay_sem.at[h, 0, i], sibling, start)

    def query_across(i, start):
        send(
            PER_HEAD + 10 + i,
            queries.at[1, 0, i],
            queries.at[1, 1, i],
            q_sem.at[1, 1, i],
            across,
            start,
        )

    def keys_on(h, i, start):
        number = PER_HEAD * h + i
        send(number + 12, kv.at[h, 0, 1, 0, i], kv.at[h, 0, 3, 0, i], far_sem.at[h, 0, i], above, start)
        block = kv.at[h, :, 1, 0, i]
        send(number + 16, block, kv.at[h, :, 1, 1, i], relay_sem.at[h, 1, i], sibling, start)

    def values_on(h, i, start):
        number = PER_HEAD * h + i
        send(number + 14, kv.at[h, 1, 2, 0, i], kv.at[h, 1, 3, 0, i], far_sem.at[h, 1, i], below, start)
        block = kv.at[h, :, 2, 0, i]
        send(number + 18, block, kv.at[h, :, 2, 1, i], relay_sem.at[h, 2, i], sibling, start)

    def far_on(h, i, start):
        block = kv.at[h, :, 3, 0, i]
        send(PER_HEAD * h + 20 + i, block, kv.at[h, :, 3, 1, i], relay_sem.at[h, 3, i], sibling, start)

    def part_across(start):
        send(PER_HEAD + 22, part_out, part_in, part_sem.at[0], across, start)

    def home(slot, start):
        head, plane = (1, y) if slot == 1 else (2 * y, y if slot == 0 else 1 - y)
        for i in range(2):
            for f in range(2):
                send(
                    PER_HEAD * slot + 23 + 2 * i + f,
                    result.at[slot, i],
                    merged.at[head, model, :, lanes(2 * half + x % 2)],
                    o_sem.at[head, model, half],
                    (f, x % 2, plane, z, 2 * core + i),
                    start,
                    True,
                )

    def hand_over(h, m, f, start):
        block = merged.at[h, m, :, lanes(2 * f + core)]
        send(PER_HEAD * h + 27 + 2 * m + f, block, block, hand_sem.at[h, m, f], sibling, start)

    last = 3 * PER_HEAD
    share = pl.ds(pl.multiple_of(SHARE * x, SHARE), SHARE)

    def weights_beside(start):
        columns = pl.ds(pl.multiple_of((2 * half + 1 - core) * WIDTH, WIDTH), WIDTH)
        send(last, base_w.at[:, columns], w_base.at[grp], w_sem.at[0], sibling, start)

    def weights_across(start):
        for c in range(2):
            columns = pl.ds(pl.multiple_of((2 * (1 - half) + c) * WIDTH, WIDTH), WIDTH)
            send(
                last + 1 + c,
                base_w.at[share, columns],
                w_base.at[grp, share],
                w_sem.at[1 + core],
                (1 - half, c, y, z, x),
                start,
            )

    def weights_along(start):
        for d in range(1, 4):
            block = w_base.at[pl.ds(2 * (1 - half), 2), share]
            send(
                last + 2 + d, block, block, w_sem.at[2 + d], (half, core, y, z, (x + d) % 4), start
            )

    near = jnp.where(x // 2 == core, x % 2, 1 - x % 2)

    def blocks_in(h):
        for i in (near, 1 - near):
            arrive(kv.at[h, :, 0, 0, i], x_sem.at[h, i])
            ring_out(h, i, True)

    def queries_in(group, side):
        for i in range(2):
            arrive(queries.at[group, side, i], q_sem.at[group, side, i])

    def neighbours_in(h):
        for i in (near, 1 - near):
            arrive(kv.at[h, :, 1, 0, i], z_sem.at[h, 0, i])
            keys_on(h, i, True)
            arrive(kv.at[h, :, 2, 0, i], z_sem.at[h, 1, i])
            values_on(h, i, True)

    def far_in(h):
        for i in (near, 1 - near):
            for j in range(2):
                arrive(kv.at[h, j, 3, 0, i], far_sem.at[h, j, i])
            far_on(h, i, True)

    def relayed(h, block):
        for i in range(2):
            arrive(kv.at[h, :, block, 1, i], relay_sem.at[h, block, i])

    def update(h, low, count, sides=(0, 1)):
        group = h % 2
        keys = kv[h, 0, low : low + count].reshape(count * 4 * ROWS, HD)
        values = kv[h, 1, low : low + count].reshape(count * 4 * ROWS, HD)
        values = jnp.concatenate([values, jnp.ones_like(values)], axis=1)
        for side in sides:
            for i in range(2):
                scores = lax.dot_general(
                    queries[group, side, i], keys, NT, preferred_element_type=jnp.float32
                )
                old = best[group, side, i][:, :1]
                new = jnp.maximum(old, jnp.max(scores, axis=1, keepdims=True))
                weights = jnp.exp2(scores * SCALE - new * SCALE).astype(jnp.bfloat16)
                keep = jnp.exp2((old - new) * SCALE)
                best[group, side, i] = jnp.broadcast_to(new, best.shape[3:])
                accum[group, side, i] = accum[group, side, i] * keep + jnp.dot(
                    weights, values, preferred_element_type=jnp.float32
                )

    lane = lax.broadcasted_iota(jnp.int32, (ROWS, HD), 1)

    def outcome(side, i):
        total = accum[1, side, i][:, HD:]
        return accum[1, side, i][:, :HD] / total, best[1, side, i] * SCALE + jnp.log2(total)

    def part():
        packed = jnp.zeros((ROWS, HD), jnp.float32)
        for i in range(2):
            value, rest = outcome(1, i)
            part_out[i] = value.astype(jnp.bfloat16)
            for j in range(3):
                piece = rest.astype(jnp.bfloat16).astype(jnp.float32)
                packed = jnp.where(lane == 3 * i + j, piece, packed)
                rest = rest - piece
        part_out[2] = packed.astype(jnp.bfloat16)
        part_across(True)

    def combine():
        arrive(part_in, part_sem.at[0])
        packed = part_in[2].astype(jnp.float32)
        for i in range(2):
            value, log_sum = outcome(0, i)
            other = (
                packed[:, 3 * i : 3 * i + 1]
                + packed[:, 3 * i + 1 : 3 * i + 2]
                + packed[:, 3 * i + 2 : 3 * i + 3]
            )
            top = jnp.maximum(log_sum, other)
            mine = jnp.exp2(log_sum - top)
            theirs = jnp.exp2(other - top)
            mixed = value * mine + part_in[i].astype(jnp.float32) * theirs
            result[1, i] = (mixed / (mine + theirs)).astype(jnp.bfloat16)
        home(1, True)

    def whole(slot):
        for i in range(2):
            done = accum[0, slot // 2, i]
            result[slot, i] = (done[:, :HD] / done[:, HD:]).astype(jnp.bfloat16)
        home(slot, True)

    def results_in(h):
        for m in range(2):
            for f in range(2):
                arrive(merged.at[h, m, :, lanes(2 * f + core)], o_sem.at[h, m, f])
                hand_over(h, m, f, True)

    def project(h):
        for m in range(2):
            for f in range(2):
                arrive(merged.at[h, m, :, lanes(2 * f + 1 - core)], hand_sem.at[h, m, f])
        for m, weight in ((0, w_control), (1, w_base)):
            rows = weight[:, h * HD : (h + 1) * HD].reshape(4 * HD, WIDTH)
            term = jnp.dot(merged[h, m], rows, preferred_element_type=jnp.float32)
            proj[m] = term if h == 1 else proj[m] + term

    pairs_out(0, True)
    queries_out(0, True)
    queries_out(2, True)
    pairs_out(1, True)
    queries_out(1, True)
    pairs_out(2, True)
    weights_beside(True)
    for copy in locals_in:
        copy.start()
    best[...] = jnp.full(best.shape, NEG, jnp.float32)
    accum[...] = jnp.zeros(accum.shape, jnp.float32)
    blocks_in(0)

    def slot_step(h, carry):
        relayed(h, 0)

        @pl.when(h == 0)
        def _():
            queries_in(0, 0)

        queries_in(h, 1)
        update(h, 0, 1)

        @pl.when(h == 0)
        def _():
            blocks_in(1)
            neighbours_in(0)
            queries_in(1, 0)
            for i in range(2):
                query_across(i, True)
            weights_across(True)

        relayed(h, 1)
        relayed(h, 2)
        update(h, 1, 2)

        @pl.when(h == 0)
        def _():
            blocks_in(2)

        far_in(h)
        neighbours_in(h + 1)
        relayed(h, 3)
        update(h, 3, 1)
        return carry

    lax.fori_loop(0, 2, slot_step, 0)
    part()
    for c in range(2):
        arrive(w_base.at[2 * (1 - half) + c, share], w_sem.at[1 + c])
    weights_along(True)
    relayed(2, 0)
    update(2, 0, 1)
    far_in(2)
    relayed(2, 1)
    update(2, 1, 1)
    combine()
    relayed(2, 2)
    relayed(2, 3)
    update(2, 2, 2, (1,))
    whole(2)
    update(2, 2, 2, (0,))
    whole(0)

    results_in(1)
    for copy in locals_in:
        copy.wait()
    arrive(w_base.at[2 * half + 1 - core], w_sem.at[0])
    for d in range(1, 4):
        rows = pl.ds(pl.multiple_of(SHARE * ((x + 4 - d) % 4), SHARE), SHARE)
        arrive(w_base.at[pl.ds(2 * (1 - half), 2), rows], w_sem.at[2 + d])
    project(1)
    results_in(0)
    results_in(2)
    project(0)
    project(2)

    for k in range(WIDTH // HD):
        part_lanes = slice(k * HD, (k + 1) * HD)
        row = pl.ds(grp * (WIDTH // HD) + k, 1)
        first = x_control[:, part_lanes].astype(jnp.float32) + control_gate[row, :] * proj[0, :, part_lanes]
        first = first.astype(jnp.bfloat16)
        control_out[:, part_lanes] = first
        second = x_base[:, part_lanes].astype(jnp.float32) + base_gate[row, :] * proj[1, :, part_lanes]
        base_out[:, part_lanes] = (second + first.astype(jnp.float32)).astype(jnp.bfloat16)

    for h in range(3):
        pairs_out(h, False)
        queries_out(h, False)
        home(h, False)

    def finish(h, carry):
        for i in range(2):
            ring_out(h, i, False)
            keys_on(h, i, False)
            values_on(h, i, False)
            far_on(h, i, False)
        for m in range(2):
            for f in range(2):
                hand_over(h, m, f, False)
        return carry

    lax.fori_loop(0, 3, finish, 0)
    for i in range(2):
        query_across(i, False)
    part_across(False)
    weights_beside(False)
    weights_across(False)
    weights_along(False)


def on_device(
    control_x, control_qkv, control_out_w, control_gate, base_x, base_qkv, base_out_w, base_gate
):
    vmem = pl.BlockSpec(memory_space=pltpu.VMEM)
    anywhere = pl.BlockSpec(memory_space=pl.ANY)
    dma = pltpu.SemaphoreType.DMA
    half16 = jnp.bfloat16
    full32 = jnp.float32
    shape = jax.ShapeDtypeStruct((ROWS, WIDTH), half16)
    return pl.pallas_call(
        sublayer_kernel,
        out_shape=(shape, shape),
        in_specs=[anywhere, anywhere, anywhere, vmem, anywhere, anywhere, anywhere, vmem],
        out_specs=(vmem, vmem),
        scratch_shapes=[
            pltpu.VMEM((3, 2, 4, 2, 2, ROWS, HD), half16),
            pltpu.VMEM((2, 2, 2, ROWS, HD), half16),
            pltpu.VMEM((2, 2, 2, ROWS, HD), full32),
            pltpu.VMEM((2, 2, 2, ROWS, 2 * HD), full32),
            pltpu.VMEM((3, ROWS, HD), half16),
            pltpu.VMEM((3, ROWS, HD), half16),
            pltpu.VMEM((3, 2, ROWS, HD), half16),
            pltpu.VMEM((3, 2, ROWS, 4 * HD), half16),
            pltpu.VMEM((4, GROUP, WIDTH), half16),
            pltpu.VMEM((4, GROUP, WIDTH), half16),
            pltpu.VMEM((2, ROWS, WIDTH), full32),
            pltpu.VMEM((ROWS, WIDTH), half16),
            pltpu.VMEM((ROWS, WIDTH), half16),
            dma((3, 2)),
            dma((2, 2, 2)),
            dma((3, 2, 2)),
            dma((3, 2, 2)),
            dma((3, 4, 2)),
            dma((1,)),
            dma((3, 2, 2)),
            dma((3, 2, 2)),
            dma((6,)),
            dma((4,)),
            dma((3 * PER_HEAD + 6,)),
        ],
        compiler_params=pltpu.CompilerParams(
            collective_id=0, has_side_effects=True, vmem_limit_bytes=60 * 2**20
        ),
        name="sublayer",
    )(
        control_x,
        control_qkv.transpose(1, 0, 2),
        control_out_w.reshape(4, GROUP, 4 * WIDTH),
        control_gate.reshape(4 * WIDTH // HD, HD),
        base_x,
        base_qkv.transpose(1, 0, 2),
        base_out_w,
        base_gate.reshape(4 * WIDTH // HD, HD),
    )


def solution(mesh):
    in_specs = (
        P("seq", None),
        P("seq", None, None),
        P(),
        P(),
        P("seq", "grp"),
        P("seq", None, "grp"),
        P("grp", None),
        P(),
    )
    out_specs = (P("seq", "grp"), P("seq", "grp"))
    return jax.shard_map(
        on_device, mesh=mesh, in_specs=in_specs, out_specs=out_specs, check_vma=False
    )
```

```python
import math

import jax
import jax.numpy as jnp
from jax import lax
from jax.experimental import pallas as pl
from jax.experimental.pallas import tpu as pltpu
from jax.sharding import PartitionSpec as P

HD = 128
ROWS = 320
WIDTH = 768
GROUP = 3 * HD
SHARE = GROUP // 4
SCALE = 1.4426950408889634 / math.sqrt(HD)
NEG = -1e30
NT = (((1,), (1,)), ((), ()))
PER_HEAD = 31


def sublayer_kernel(
    control_x,
    control,
    control_w,
    control_gate,
    base_x,
    base,
    base_w,
    base_gate,
    outs,
    kv,
    queries,
    best,
    accum,
    part_out,
    part_in,
    result,
    merged,
    w_control,
    w_base,
    proj,
    x_control,
    x_base,
    x_sem,
    q_sem,
    z_sem,
    far_sem,
    relay_sem,
    part_sem,
    o_sem,
    hand_sem,
    w_sem,
    local_sem,
    send_sem,
):
    grp = lax.axis_index("grp")
    seq = lax.axis_index("seq")
    half, core, y, z, x = grp // 2, grp % 2, seq // 16, (seq // 4) % 4, seq % 4
    here = (half, core, y, z, x)
    sibling = (half, 1 - core, y, z, x)
    above = (half, core, y, (z + 1) % 4, x)
    below = (half, core, y, (z + 3) % 4, x)
    right = (half, core, y, z, (x + 1) % 4)
    left = (half, core, y, z, (x + 3) % 4)
    across = (half, core, 1 - y, z, x)

    def ident(device):
        return {"grp": 2 * device[0] + device[1], "seq": 16 * device[2] + 4 * device[3] + device[4]}

    barrier = pltpu.get_barrier_semaphore()
    greeted = (
        [sibling, above, below, right, left, across, (half, core, y, z, (x + 2) % 4)]
        + [(half, x % 2, p, z, 2 * core + i) for i in range(2) for p in (y, 1 - y)]
        + [(half, z % 2, y, 2 * core + i, x) for i in range(2)]
        + [(f, x // 2, p, z, 2 * m + core) for f in range(2) for m in range(2) for p in (y, 1 - y)]
        + [(f, z // 2, y, 2 * m + core, x) for f in range(2) for m in range(2)]
        + [(1 - half, i, y, z, x) for i in range(2)]
    )
    for device in greeted:
        pl.semaphore_signal(barrier, inc=1, device_id=ident(device))

    lanes_out = pl.ds(pl.multiple_of(grp * WIDTH, WIDTH), WIDTH)
    locals_in = [
        pltpu.make_async_copy(control_w.at[:, :, lanes_out], w_control, local_sem.at[0]),
        pltpu.make_async_copy(base_w.at[:, lanes_out], w_base.at[grp], local_sem.at[1]),
        pltpu.make_async_copy(control_x.at[:, lanes_out], x_control, local_sem.at[2]),
        pltpu.make_async_copy(base_x, x_base, local_sem.at[3]),
    ]

    pl.semaphore_wait(barrier, len(greeted))

    def send(number, source, target, arrived, device, start, may_be_here=False):
        remote = pltpu.make_async_remote_copy(
            source, target, send_sem.at[number], arrived, device_id=ident(device)
        )
        act = remote.start if start else remote.wait_send
        if not may_be_here:
            act()
            return
        own = device[0] == here[0]
        for left, right in zip(device[1:], here[1:]):
            own = jnp.logical_and(own, left == right)
        pl.when(jnp.logical_not(own))(act)
        if start:

            @pl.when(own)
            def _():
                pltpu.make_async_copy(source, target, arrived).start()

    def arrive(ref, sem):
        pltpu.make_async_copy(ref, ref, sem).wait()

    def lanes(index):
        return pl.ds(pl.multiple_of(index * HD, HD), HD)

    def route(slot, m):
        if slot == 1:
            return 1, z % 2, (half, z // 2, y, 2 * m + core, x)
        plane = y if slot == 0 else 1 - y
        return 2 * plane, x % 2, (half, x // 2, plane, z, 2 * m + core)

    def pairs_out(slot, start):
        for m, ref, first in ((0, control, 3 * grp), (1, base, 0)):
            head, i, device = route(slot, m)
            send(
                PER_HEAD * slot + m,
                ref.at[pl.ds(1, 2), :, lanes(first + head)],
                kv.at[slot, :, 0, 0, i],
                x_sem.at[slot, i],
                device,
                start,
                True,
            )

    def queries_out(slot, start):
        for m, ref, first in ((0, control, 3 * grp), (1, base, 0)):
            head, i, device = route(slot, m)
            send(
                PER_HEAD * slot + 2 + m,
                ref.at[0, :, lanes(first + head)],
                queries.at[slot % 2, slot // 2, i],
                q_sem.at[slot % 2, slot // 2, i],
                device,
                start,
                True,
            )

    def ahead(h):
        return right if h == 1 else above

    def behind(h):
        return left if h == 1 else below

    def ring_out(h, i, start):
        block = kv.at[h, :, 0, 0, i]
        number = PER_HEAD * h + i
        send(number + 4, block, kv.at[h, :, 1, 0, i], z_sem.at[h, 0, i], ahead(h), start)
        send(number + 6, block, kv.at[h, :, 2, 0, i], z_sem.at[h, 1, i], behind(h), start)
        send(number + 8, block, kv.at[h, :, 0, 1, i], relay_sem.at[h, 0, i], sibling, start)

    def query_across(i, start):
        send(
            PER_HEAD + 10 + i,
            queries.at[1, 0, i],
            queries.at[1, 1, i],
            q_sem.at[1, 1, i],
            across,
            start,
        )

    def keys_on(h, i, start):
        number = PER_HEAD * h + i
        send(number + 12, kv.at[h, 0, 1, 0, i], kv.at[h, 0, 3, 0, i], far_sem.at[h, 0, i], ahead(h), start)
        block = kv.at[h, :, 1, 0, i]
        send(number + 16, block, kv.at[h, :, 1, 1, i], relay_sem.at[h, 1, i], sibling, start)

    def values_on(h, i, start):
        number = PER_HEAD * h + i
        send(number + 14, kv.at[h, 1, 2, 0, i], kv.at[h, 1, 3, 0, i], far_sem.at[h, 1, i], behind(h), start)
        block = kv.at[h, :, 2, 0, i]
        send(number + 18, block, kv.at[h, :, 2, 1, i], relay_sem.at[h, 2, i], sibling, start)

    def far_on(h, i, start):
        block = kv.at[h, :, 3, 0, i]
        send(PER_HEAD * h + 20 + i, block, kv.at[h, :, 3, 1, i], relay_sem.at[h, 3, i], sibling, start)

    def part_across(start):
        send(PER_HEAD + 22, part_out, part_in, part_sem.at[0], across, start)

    def home(slot, start):
        head, place = (1, z) if slot == 1 else (2 * y, x)
        for i in range(2):
            for f in range(2):
                if slot == 1:
                    owner = (f, z % 2, y, 2 * core + i, x)
                else:
                    owner = (f, x % 2, y if slot == 0 else 1 - y, z, 2 * core + i)
                send(
                    PER_HEAD * slot + 23 + 2 * i + f,
                    result.at[slot, i],
                    merged.at[head, place // 2, :, lanes(2 * half + place % 2)],
                    o_sem.at[head, place // 2, half],
                    owner,
                    start,
                    True,
                )

    def hand_over(h, m, f, start):
        block = merged.at[h, m, :, lanes(2 * f + core)]
        send(PER_HEAD * h + 27 + 2 * m + f, block, block, hand_sem.at[h, m, f], sibling, start)

    last = 3 * PER_HEAD
    share = pl.ds(pl.multiple_of(SHARE * x, SHARE), SHARE)

    def weights_beside(start):
        columns = pl.ds(pl.multiple_of((2 * half + 1 - core) * WIDTH, WIDTH), WIDTH)
        send(last, base_w.at[:, columns], w_base.at[grp], w_sem.at[0], sibling, start)

    def weights_across(start):
        for c in range(2):
            columns = pl.ds(pl.multiple_of((2 * (1 - half) + c) * WIDTH, WIDTH), WIDTH)
            send(
                last + 1 + c,
                base_w.at[share, columns],
                w_base.at[grp, share],
                w_sem.at[1 + core],
                (1 - half, c, y, z, x),
                start,
            )

    def weights_along(start):
        for d in range(1, 4):
            block = w_base.at[pl.ds(2 * (1 - half), 2), share]
            send(
                last + 2 + d, block, block, w_sem.at[2 + d], (half, core, y, z, (x + d) % 4), start
            )

    def order(h):
        place = z if h == 1 else x
        near = jnp.where(place // 2 == core, place % 2, 1 - place % 2)
        return near, 1 - near

    def blocks_in(h):
        for i in order(h):
            arrive(kv.at[h, :, 0, 0, i], x_sem.at[h, i])
            ring_out(h, i, True)

    def queries_in(group, side):
        for i in range(2):
            arrive(queries.at[group, side, i], q_sem.at[group, side, i])

    def neighbours_in(h):
        for i in order(h):
            arrive(kv.at[h, :, 1, 0, i], z_sem.at[h, 0, i])
            keys_on(h, i, True)
            arrive(kv.at[h, :, 2, 0, i], z_sem.at[h, 1, i])
            values_on(h, i, True)

    def far_in(h):
        for i in order(h):
            for j in range(2):
                arrive(kv.at[h, j, 3, 0, i], far_sem.at[h, j, i])
            far_on(h, i, True)

    def relayed(h, block):
        for i in range(2):
            arrive(kv.at[h, :, block, 1, i], relay_sem.at[h, block, i])

    def update(h, low, count, side=None):
        group = h % 2
        keys = kv[h, 0, low : low + count].reshape(count * 4 * ROWS, HD)
        values = kv[h, 1, low : low + count].reshape(count * 4 * ROWS, HD)
        values = jnp.concatenate([values, jnp.ones_like(values)], axis=1)
        if side is None:
            tiles = [(p, i, slice(0, ROWS)) for p in range(2) for i in range(2)]
        else:
            cut = ROWS // 2
            tiles = [(side, i, slice(k * cut, (k + 1) * cut)) for i in range(2) for k in range(2)]
        for p, i, rows in tiles:
            scores = lax.dot_general(
                queries[group, p, i, rows], keys, NT, preferred_element_type=jnp.float32
            )
            old = best[group, p, i, rows][:, :1]
            new = jnp.maximum(old, jnp.max(scores, axis=1, keepdims=True))
            weights = jnp.exp2(scores * SCALE - new * SCALE).astype(jnp.bfloat16)
            keep = jnp.exp2((old - new) * SCALE)
            best[group, p, i, rows] = jnp.broadcast_to(new, (new.shape[0], HD))
            accum[group, p, i, rows] = accum[group, p, i, rows] * keep + jnp.dot(
                weights, values, preferred_element_type=jnp.float32
            )

    lane = lax.broadcasted_iota(jnp.int32, (ROWS, HD), 1)

    def outcome(side, i):
        total = accum[1, side, i][:, HD:]
        return accum[1, side, i][:, :HD] / total, best[1, side, i] * SCALE + jnp.log2(total)

    def part():
        packed = jnp.zeros((ROWS, HD), jnp.float32)
        for i in range(2):
            value, rest = outcome(1, i)
            part_out[i] = value.astype(jnp.bfloat16)
            for j in range(3):
                piece = rest.astype(jnp.bfloat16).astype(jnp.float32)
                packed = jnp.where(lane == 3 * i + j, piece, packed)
                rest = rest - piece
        part_out[2] = packed.astype(jnp.bfloat16)
        part_across(True)

    def combine():
        arrive(part_in, part_sem.at[0])
        packed = part_in[2].astype(jnp.float32)
        for i in range(2):
            value, log_sum = outcome(0, i)
            other = (
                packed[:, 3 * i : 3 * i + 1]
                + packed[:, 3 * i + 1 : 3 * i + 2]
                + packed[:, 3 * i + 2 : 3 * i + 3]
            )
            top = jnp.maximum(log_sum, other)
            mine = jnp.exp2(log_sum - top)
            theirs = jnp.exp2(other - top)
            mixed = value * mine + part_in[i].astype(jnp.float32) * theirs
            result[1, i] = (mixed / (mine + theirs)).astype(jnp.bfloat16)
        home(1, True)

    def whole(slot):
        for i in range(2):
            done = accum[0, slot // 2, i]
            result[slot, i] = (done[:, :HD] / done[:, HD:]).astype(jnp.bfloat16)
        home(slot, True)

    def results_in(h):
        for m in range(2):
            for f in range(2):
                arrive(merged.at[h, m, :, lanes(2 * f + core)], o_sem.at[h, m, f])
                hand_over(h, m, f, True)

    def project(h, first=False):
        for m in range(2):
            for f in range(2):
                arrive(merged.at[h, m, :, lanes(2 * f + 1 - core)], hand_sem.at[h, m, f])
        for m, weight in ((0, w_control), (1, w_base)):
            rows = weight[:, lanes(h)].reshape(4 * HD, WIDTH)
            term = jnp.dot(merged[h, m], rows, preferred_element_type=jnp.float32)
            proj[m] = term if first else proj[m] + term

    pairs_out(0, True)
    pairs_out(1, True)
    queries_out(0, True)
    queries_out(2, True)
    queries_out(1, True)
    weights_across(True)
    pairs_out(2, True)
    weights_beside(True)
    for copy in locals_in:
        copy.start()
    best[...] = jnp.full(best.shape, NEG, jnp.float32)
    accum[...] = jnp.zeros(accum.shape, jnp.float32)
    blocks_in(0)
    blocks_in(1)
    queries_in(1, 0)
    for i in range(2):
        query_across(i, True)
    relayed(0, 0)
    queries_in(0, 0)
    queries_in(0, 1)
    update(0, 0, 1)
    blocks_in(2)
    neighbours_in(0)
    neighbours_in(1)
    relayed(0, 1)
    relayed(0, 2)
    update(0, 1, 2)
    far_in(0)
    far_in(1)
    for c in range(2):
        arrive(w_base.at[2 * (1 - half) + c, share], w_sem.at[1 + c])
    weights_along(True)
    relayed(0, 3)
    update(0, 3, 1)
    neighbours_in(2)
    queries_in(1, 1)
    relayed(1, 0)
    relayed(1, 1)
    update(1, 0, 2)
    far_in(2)
    relayed(1, 2)
    relayed(1, 3)
    update(1, 2, 2)
    part()
    for block in range(4):
        relayed(2, block)
    update(2, 0, 2, 1)
    update(2, 2, 2, 1)
    whole(2)
    combine()
    update(2, 0, 2, 0)
    update(2, 2, 2, 0)
    whole(0)

    for h in range(3):
        pairs_out(h, False)
        queries_out(h, False)
        for i in range(2):
            ring_out(h, i, False)
            keys_on(h, i, False)
            values_on(h, i, False)
            far_on(h, i, False)
    for i in range(2):
        query_across(i, False)
    part_across(False)
    weights_beside(False)
    weights_across(False)
    weights_along(False)
    for copy in locals_in:
        copy.wait()
    arrive(w_base.at[2 * half + 1 - core], w_sem.at[0])
    for d in range(1, 4):
        rows = pl.ds(pl.multiple_of(SHARE * ((x + 4 - d) % 4), SHARE), SHARE)
        arrive(w_base.at[pl.ds(2 * (1 - half), 2), rows], w_sem.at[2 + d])
    results_in(1)
    project(1, True)
    results_in(2 * (1 - y))
    project(2 * (1 - y))
    results_in(2 * y)
    project(2 * y)

    for k in range(WIDTH // HD):
        part_lanes = slice(k * HD, (k + 1) * HD)
        row = pl.ds(grp * (WIDTH // HD) + k, 1)
        first = x_control[:, part_lanes].astype(jnp.float32) + control_gate[row, :] * proj[0, :, part_lanes]
        first = first.astype(jnp.bfloat16)
        outs[0, :, part_lanes] = first
        second = x_base[:, part_lanes].astype(jnp.float32) + base_gate[row, :] * proj[1, :, part_lanes]
        outs[1, :, part_lanes] = (second + first.astype(jnp.float32)).astype(jnp.bfloat16)

    for h in range(3):
        home(h, False)
        for m in range(2):
            for f in range(2):
                hand_over(h, m, f, False)


def on_device(
    control_x, control_qkv, control_out_w, control_gate, base_x, base_qkv, base_out_w, base_gate
):
    vmem = pl.BlockSpec(memory_space=pltpu.VMEM)
    anywhere = pl.BlockSpec(memory_space=pl.ANY)
    dma = pltpu.SemaphoreType.DMA
    half16 = jnp.bfloat16
    full32 = jnp.float32
    outs = pl.pallas_call(
        sublayer_kernel,
        out_shape=jax.ShapeDtypeStruct((2, ROWS, WIDTH), half16),
        in_specs=[anywhere, anywhere, anywhere, vmem, anywhere, anywhere, anywhere, vmem],
        out_specs=vmem,
        scratch_shapes=[
            pltpu.VMEM((3, 2, 4, 2, 2, ROWS, HD), half16),
            pltpu.VMEM((2, 2, 2, ROWS, HD), half16),
            pltpu.VMEM((2, 2, 2, ROWS, HD), full32),
            pltpu.VMEM((2, 2, 2, ROWS, 2 * HD), full32),
            pltpu.VMEM((3, ROWS, HD), half16),
            pltpu.VMEM((3, ROWS, HD), half16),
            pltpu.VMEM((3, 2, ROWS, HD), half16),
            pltpu.VMEM((3, 2, ROWS, 4 * HD), half16),
            pltpu.VMEM((4, GROUP, WIDTH), half16),
            pltpu.VMEM((4, GROUP, WIDTH), half16),
            pltpu.VMEM((2, ROWS, WIDTH), full32),
            pltpu.VMEM((ROWS, WIDTH), half16),
            pltpu.VMEM((ROWS, WIDTH), half16),
            dma((3, 2)),
            dma((2, 2, 2)),
            dma((3, 2, 2)),
            dma((3, 2, 2)),
            dma((3, 4, 2)),
            dma((1,)),
            dma((3, 2, 2)),
            dma((3, 2, 2)),
            dma((6,)),
            dma((4,)),
            dma((3 * PER_HEAD + 6,)),
        ],
        compiler_params=pltpu.CompilerParams(
            collective_id=0, has_side_effects=True, vmem_limit_bytes=60 * 2**20
        ),
        name="sublayer",
    )(
        control_x,
        control_qkv.transpose(1, 0, 2),
        control_out_w.reshape(4, GROUP, 4 * WIDTH),
        control_gate.reshape(4 * WIDTH // HD, HD),
        base_x,
        base_qkv.transpose(1, 0, 2),
        base_out_w,
        base_gate.reshape(4 * WIDTH // HD, HD),
    )
    return outs[0], outs[1]


def solution(mesh):
    in_specs = (
        P("seq", None),
        P("seq", None, None),
        P(),
        P(),
        P("seq", "grp"),
        P("seq", None, "grp"),
        P("grp", None),
        P(),
    )
    out_specs = (P("seq", "grp"), P("seq", "grp"))
    return jax.shard_map(
        on_device, mesh=mesh, in_specs=in_specs, out_specs=out_specs, check_vma=False
    )
```

```python
import math

import jax
import jax.numpy as jnp
from jax import lax
from jax.experimental import pallas as pl
from jax.experimental.pallas import tpu as pltpu
from jax.sharding import PartitionSpec as P

HD = 128
ROWS = 320
WIDTH = 768
GROUP = 3 * HD
SHARE = GROUP // 4
SCALE = 1.4426950408889634 / math.sqrt(HD)
NEG = -1e30
NT = (((1,), (1,)), ((), ()))
PER_HEAD = 31


def sublayer_kernel(
    control_x,
    control,
    control_w,
    control_gate,
    base_x,
    base,
    base_w,
    base_gate,
    outs,
    kv,
    queries,
    best,
    accum,
    part_out,
    part_in,
    result,
    merged,
    w_control,
    w_base,
    proj,
    x_control,
    x_base,
    x_sem,
    q_sem,
    z_sem,
    far_sem,
    relay_sem,
    part_sem,
    o_sem,
    hand_sem,
    w_sem,
    local_sem,
    send_sem,
):
    grp = lax.axis_index("grp")
    seq = lax.axis_index("seq")
    half, core, y, z, x = grp // 2, grp % 2, seq // 16, (seq // 4) % 4, seq % 4
    here = (half, core, y, z, x)
    sibling = (half, 1 - core, y, z, x)
    above = (half, core, y, (z + 1) % 4, x)
    below = (half, core, y, (z + 3) % 4, x)
    right = (half, core, y, z, (x + 1) % 4)
    left = (half, core, y, z, (x + 3) % 4)
    across = (half, core, 1 - y, z, x)

    def ident(device):
        return {"grp": 2 * device[0] + device[1], "seq": 16 * device[2] + 4 * device[3] + device[4]}

    barrier = pltpu.get_barrier_semaphore()
    greeted = (
        [sibling, above, below, right, left, across, (half, core, y, z, (x + 2) % 4)]
        + [(half, x % 2, p, z, 2 * core + i) for i in range(2) for p in (y, 1 - y)]
        + [(half, z % 2, y, 2 * core + i, x) for i in range(2)]
        + [(f, x // 2, p, z, 2 * m + core) for f in range(2) for m in range(2) for p in (y, 1 - y)]
        + [(f, z // 2, y, 2 * m + core, x) for f in range(2) for m in range(2)]
        + [(1 - half, i, y, z, x) for i in range(2)]
    )
    for device in greeted:
        pl.semaphore_signal(barrier, inc=1, device_id=ident(device))

    lanes_out = pl.ds(pl.multiple_of(grp * WIDTH, WIDTH), WIDTH)
    locals_in = [
        pltpu.make_async_copy(control_w.at[:, :, lanes_out], w_control, local_sem.at[0]),
        pltpu.make_async_copy(base_w.at[:, lanes_out], w_base.at[grp], local_sem.at[1]),
        pltpu.make_async_copy(control_x.at[:, lanes_out], x_control, local_sem.at[2]),
        pltpu.make_async_copy(base_x, x_base, local_sem.at[3]),
    ]

    pl.semaphore_wait(barrier, len(greeted))

    def send(number, source, target, arrived, device, start, may_be_here=False):
        remote = pltpu.make_async_remote_copy(
            source, target, send_sem.at[number], arrived, device_id=ident(device)
        )
        act = remote.start if start else remote.wait_send
        if not may_be_here:
            act()
            return
        own = device[0] == here[0]
        for left, right in zip(device[1:], here[1:]):
            own = jnp.logical_and(own, left == right)
        pl.when(jnp.logical_not(own))(act)
        if start:

            @pl.when(own)
            def _():
                pltpu.make_async_copy(source, target, arrived).start()

    def arrive(ref, sem):
        pltpu.make_async_copy(ref, ref, sem).wait()

    def lanes(index):
        return pl.ds(pl.multiple_of(index * HD, HD), HD)

    def route(slot, m):
        if slot == 1:
            return 1, z % 2, (half, z // 2, y, 2 * m + core, x)
        plane = y if slot == 0 else 1 - y
        return 2 * plane, x % 2, (half, x // 2, plane, z, 2 * m + core)

    def pairs_out(slot, start):
        for m, ref, first in ((0, control, 3 * grp), (1, base, 0)):
            head, i, device = route(slot, m)
            send(
                PER_HEAD * slot + m,
                ref.at[pl.ds(1, 2), :, lanes(first + head)],
                kv.at[slot, :, 0, 0, i],
                x_sem.at[slot, i],
                device,
                start,
                True,
            )

    def queries_out(slot, start):
        for m, ref, first in ((0, control, 3 * grp), (1, base, 0)):
            head, i, device = route(slot, m)
            send(
                PER_HEAD * slot + 2 + m,
                ref.at[0, :, lanes(first + head)],
                queries.at[slot % 2, slot // 2, i],
                q_sem.at[slot % 2, slot // 2, i],
                device,
                start,
                True,
            )

    def ahead(h):
        return right if h == 1 else above

    def behind(h):
        return left if h == 1 else below

    def ring_out(h, i, start):
        block = kv.at[h, :, 0, 0, i]
        number = PER_HEAD * h + i
        send(number + 4, block, kv.at[h, :, 1, 0, i], z_sem.at[h, 0, i], ahead(h), start)
        send(number + 6, block, kv.at[h, :, 2, 0, i], z_sem.at[h, 1, i], behind(h), start)
        send(number + 8, block, kv.at[h, :, 0, 1, i], relay_sem.at[h, 0, i], sibling, start)

    def query_across(i, start):
        send(
            PER_HEAD + 10 + i,
            queries.at[1, 0, i],
            queries.at[1, 1, i],
            q_sem.at[1, 1, i],
            across,
            start,
        )

    def keys_on(h, i, start):
        number = PER_HEAD * h + i
        send(number + 12, kv.at[h, 0, 1, 0, i], kv.at[h, 0, 3, 0, i], far_sem.at[h, 0, i], ahead(h), start)
        block = kv.at[h, :, 1, 0, i]
        send(number + 16, block, kv.at[h, :, 1, 1, i], relay_sem.at[h, 1, i], sibling, start)

    def values_on(h, i, start):
        number = PER_HEAD * h + i
        send(number + 14, kv.at[h, 1, 2, 0, i], kv.at[h, 1, 3, 0, i], far_sem.at[h, 1, i], behind(h), start)
        block = kv.at[h, :, 2, 0, i]
        send(number + 18, block, kv.at[h, :, 2, 1, i], relay_sem.at[h, 2, i], sibling, start)

    def far_on(h, i, start):
        block = kv.at[h, :, 3, 0, i]
        send(PER_HEAD * h + 20 + i, block, kv.at[h, :, 3, 1, i], relay_sem.at[h, 3, i], sibling, start)

    def part_across(start):
        send(PER_HEAD + 22, part_out, part_in, part_sem.at[0], across, start)

    def home(slot, start):
        head, place = (1, z) if slot == 1 else (2 * y, x)
        for i in range(2):
            for f in range(2):
                if slot == 1:
                    owner = (f, z % 2, y, 2 * core + i, x)
                else:
                    owner = (f, x % 2, y if slot == 0 else 1 - y, z, 2 * core + i)
                send(
                    PER_HEAD * slot + 23 + 2 * i + f,
                    result.at[slot, i],
                    merged.at[head, place // 2, :, lanes(2 * half + place % 2)],
                    o_sem.at[head, place // 2, half],
                    owner,
                    start,
                    True,
                )

    def hand_over(h, m, f, start):
        block = merged.at[h, m, :, lanes(2 * f + core)]
        send(PER_HEAD * h + 27 + 2 * m + f, block, block, hand_sem.at[h, m, f], sibling, start)

    last = 3 * PER_HEAD
    share = pl.ds(pl.multiple_of(SHARE * x, SHARE), SHARE)

    def weights_beside(start):
        columns = pl.ds(pl.multiple_of((2 * half + 1 - core) * WIDTH, WIDTH), WIDTH)
        send(last, base_w.at[:, columns], w_base.at[grp], w_sem.at[0], sibling, start)

    def weights_across(start):
        for c in range(2):
            columns = pl.ds(pl.multiple_of((2 * (1 - half) + c) * WIDTH, WIDTH), WIDTH)
            send(
                last + 1 + c,
                base_w.at[share, columns],
                w_base.at[grp, share],
                w_sem.at[1 + core],
                (1 - half, c, y, z, x),
                start,
            )

    def weights_along(start):
        for d in range(1, 4):
            block = w_base.at[pl.ds(2 * (1 - half), 2), share]
            send(
                last + 2 + d, block, block, w_sem.at[2 + d], (half, core, y, z, (x + d) % 4), start
            )

    def order(h):
        place = z if h == 1 else x
        near = jnp.where(place // 2 == core, place % 2, 1 - place % 2)
        return near, 1 - near

    def blocks_in(h):
        for i in order(h):
            arrive(kv.at[h, :, 0, 0, i], x_sem.at[h, i])
            ring_out(h, i, True)

    def queries_in(group, side):
        for i in range(2):
            arrive(queries.at[group, side, i], q_sem.at[group, side, i])

    def neighbours_in(h):
        for i in order(h):
            arrive(kv.at[h, :, 1, 0, i], z_sem.at[h, 0, i])
            keys_on(h, i, True)
            arrive(kv.at[h, :, 2, 0, i], z_sem.at[h, 1, i])
            values_on(h, i, True)

    def far_in(h):
        for i in order(h):
            for j in range(2):
                arrive(kv.at[h, j, 3, 0, i], far_sem.at[h, j, i])
            far_on(h, i, True)

    def relayed(h, block):
        for i in range(2):
            arrive(kv.at[h, :, block, 1, i], relay_sem.at[h, block, i])

    def update(h, low, count, side=None):
        group = h % 2
        keys = kv[h, 0, low : low + count].reshape(count * 4 * ROWS, HD)
        values = kv[h, 1, low : low + count].reshape(count * 4 * ROWS, HD)
        values = jnp.concatenate([values, jnp.ones_like(values)], axis=1)
        if side is None:
            tiles = [(p, i, slice(0, ROWS)) for p in range(2) for i in range(2)]
        else:
            cut = ROWS // 2
            tiles = [(side, i, slice(k * cut, (k + 1) * cut)) for i in range(2) for k in range(2)]
        for p, i, rows in tiles:
            scores = lax.dot_general(
                queries[group, p, i, rows], keys, NT, preferred_element_type=jnp.float32
            )
            old = best[group, p, i, rows][:, :1]
            new = jnp.maximum(old, jnp.max(scores, axis=1, keepdims=True))
            weights = jnp.exp2(scores * SCALE - new * SCALE).astype(jnp.bfloat16)
            keep = jnp.exp2((old - new) * SCALE)
            best[group, p, i, rows] = jnp.broadcast_to(new, (new.shape[0], HD))
            accum[group, p, i, rows] = accum[group, p, i, rows] * keep + jnp.dot(
                weights, values, preferred_element_type=jnp.float32
            )

    lane = lax.broadcasted_iota(jnp.int32, (ROWS, HD), 1)

    def outcome(side, i):
        total = accum[1, side, i][:, HD:]
        return accum[1, side, i][:, :HD] / total, best[1, side, i] * SCALE + jnp.log2(total)

    def part():
        packed = jnp.zeros((ROWS, HD), jnp.float32)
        for i in range(2):
            value, rest = outcome(1, i)
            part_out[i] = value.astype(jnp.bfloat16)
            for j in range(3):
                piece = rest.astype(jnp.bfloat16).astype(jnp.float32)
                packed = jnp.where(lane == 3 * i + j, piece, packed)
                rest = rest - piece
        part_out[2] = packed.astype(jnp.bfloat16)
        part_across(True)

    def combine():
        arrive(part_in, part_sem.at[0])
        packed = part_in[2].astype(jnp.float32)
        for i in range(2):
            value, log_sum = outcome(0, i)
            other = (
                packed[:, 3 * i : 3 * i + 1]
                + packed[:, 3 * i + 1 : 3 * i + 2]
                + packed[:, 3 * i + 2 : 3 * i + 3]
            )
            top = jnp.maximum(log_sum, other)
            mine = jnp.exp2(log_sum - top)
            theirs = jnp.exp2(other - top)
            mixed = value * mine + part_in[i].astype(jnp.float32) * theirs
            result[1, i] = (mixed / (mine + theirs)).astype(jnp.bfloat16)
        home(1, True)

    def whole(slot):
        for i in range(2):
            done = accum[0, slot // 2, i]
            result[slot, i] = (done[:, :HD] / done[:, HD:]).astype(jnp.bfloat16)
        home(slot, True)

    def results_in(h):
        for m in range(2):
            for f in range(2):
                arrive(merged.at[h, m, :, lanes(2 * f + core)], o_sem.at[h, m, f])
                hand_over(h, m, f, True)

    def handed(h):
        for m in range(2):
            for f in range(2):
                arrive(merged.at[h, m, :, lanes(2 * f + 1 - core)], hand_sem.at[h, m, f])

    def term(h, m, columns):
        weight = (w_control, w_base)[m]
        rows = weight[:, lanes(h), columns].reshape(4 * HD, -1)
        return jnp.dot(merged[h, m], rows, preferred_element_type=jnp.float32)

    def project(h, first=False):
        handed(h)
        for m in range(2):
            new = term(h, m, slice(None))
            proj[m] = new if first else proj[m] + new

    pairs_out(0, True)
    pairs_out(1, True)
    queries_out(0, True)
    queries_out(2, True)
    queries_out(1, True)
    weights_across(True)
    pairs_out(2, True)
    weights_beside(True)
    for copy in locals_in:
        copy.start()
    best[...] = jnp.full(best.shape, NEG, jnp.float32)
    accum[...] = jnp.zeros(accum.shape, jnp.float32)
    blocks_in(0)
    blocks_in(1)
    queries_in(1, 0)
    for i in range(2):
        query_across(i, True)
    relayed(0, 0)
    queries_in(0, 0)
    queries_in(0, 1)
    update(0, 0, 1)
    blocks_in(2)
    relayed(1, 0)
    queries_in(1, 1)
    update(1, 0, 1)
    neighbours_in(0)
    relayed(0, 1)
    update(0, 1, 1)
    neighbours_in(1)
    relayed(0, 2)
    update(0, 2, 1)
    far_in(0)
    relayed(1, 1)
    update(1, 1, 1)
    far_in(1)
    for c in range(2):
        arrive(w_base.at[2 * (1 - half) + c, share], w_sem.at[1 + c])
    weights_along(True)
    relayed(0, 3)
    update(0, 3, 1)
    neighbours_in(2)
    relayed(1, 2)
    update(1, 2, 1)
    relayed(1, 3)
    update(1, 3, 1)
    part()
    far_in(2)
    relayed(2, 0)
    relayed(2, 1)
    update(2, 0, 2)
    combine()
    relayed(2, 2)
    relayed(2, 3)
    update(2, 2, 2, 1)
    whole(2)
    update(2, 2, 2, 0)
    whole(0)

    for h in range(3):
        pairs_out(h, False)
        queries_out(h, False)
        for i in range(2):
            ring_out(h, i, False)
            keys_on(h, i, False)
            values_on(h, i, False)
            far_on(h, i, False)
    for i in range(2):
        query_across(i, False)
    part_across(False)
    weights_beside(False)
    weights_across(False)
    weights_along(False)
    for copy in locals_in:
        copy.wait()
    arrive(w_base.at[2 * half + 1 - core], w_sem.at[0])
    for d in range(1, 4):
        rows = pl.ds(pl.multiple_of(SHARE * ((x + 4 - d) % 4), SHARE), SHARE)
        arrive(w_base.at[pl.ds(2 * (1 - half), 2), rows], w_sem.at[2 + d])
    results_in(1)
    project(1, True)
    results_in(2 * (1 - y))
    project(2 * (1 - y))
    results_in(2 * y)
    handed(2 * y)
    per_row = WIDTH // HD
    for k in range(3):
        columns = slice(2 * k * HD, (2 * k + 2) * HD)
        gates = [
            jnp.concatenate([gate[pl.ds(grp * per_row + 2 * k + j, 1), :] for j in range(2)], axis=1)
            for gate in (control_gate, base_gate)
        ]
        sums = [proj[m, :, columns] + term(2 * y, m, columns) for m in range(2)]
        first = (x_control[:, columns].astype(jnp.float32) + gates[0] * sums[0]).astype(jnp.bfloat16)
        outs[0, :, columns] = first
        second = x_base[:, columns].astype(jnp.float32) + gates[1] * sums[1]
        outs[1, :, columns] = (second + first.astype(jnp.float32)).astype(jnp.bfloat16)

    for h in range(3):
        home(h, False)
        for m in range(2):
            for f in range(2):
                hand_over(h, m, f, False)


def on_device(
    control_x, control_qkv, control_out_w, control_gate, base_x, base_qkv, base_out_w, base_gate
):
    vmem = pl.BlockSpec(memory_space=pltpu.VMEM)
    anywhere = pl.BlockSpec(memory_space=pl.ANY)
    dma = pltpu.SemaphoreType.DMA
    half16 = jnp.bfloat16
    full32 = jnp.float32
    outs = pl.pallas_call(
        sublayer_kernel,
        out_shape=jax.ShapeDtypeStruct((2, ROWS, WIDTH), half16),
        in_specs=[anywhere, anywhere, anywhere, vmem, anywhere, anywhere, anywhere, vmem],
        out_specs=vmem,
        scratch_shapes=[
            pltpu.VMEM((3, 2, 4, 2, 2, ROWS, HD), half16),
            pltpu.VMEM((2, 2, 2, ROWS, HD), half16),
            pltpu.VMEM((2, 2, 2, ROWS, HD), full32),
            pltpu.VMEM((2, 2, 2, ROWS, 2 * HD), full32),
            pltpu.VMEM((3, ROWS, HD), half16),
            pltpu.VMEM((3, ROWS, HD), half16),
            pltpu.VMEM((3, 2, ROWS, HD), half16),
            pltpu.VMEM((3, 2, ROWS, 4 * HD), half16),
            pltpu.VMEM((4, GROUP, WIDTH), half16),
            pltpu.VMEM((4, GROUP, WIDTH), half16),
            pltpu.VMEM((2, ROWS, WIDTH), full32),
            pltpu.VMEM((ROWS, WIDTH), half16),
            pltpu.VMEM((ROWS, WIDTH), half16),
            dma((3, 2)),
            dma((2, 2, 2)),
            dma((3, 2, 2)),
            dma((3, 2, 2)),
            dma((3, 4, 2)),
            dma((1,)),
            dma((3, 2, 2)),
            dma((3, 2, 2)),
            dma((6,)),
            dma((4,)),
            dma((3 * PER_HEAD + 6,)),
        ],
        compiler_params=pltpu.CompilerParams(
            collective_id=0, has_side_effects=True, vmem_limit_bytes=60 * 2**20
        ),
        name="sublayer",
    )(
        control_x,
        control_qkv.transpose(1, 0, 2),
        control_out_w.reshape(4, GROUP, 4 * WIDTH),
        control_gate.reshape(4 * WIDTH // HD, HD),
        base_x,
        base_qkv.transpose(1, 0, 2),
        base_out_w,
        base_gate.reshape(4 * WIDTH // HD, HD),
    )
    return outs[0], outs[1]


def solution(mesh):
    in_specs = (
        P("seq", None),
        P("seq", None, None),
        P(),
        P(),
        P("seq", "grp"),
        P("seq", None, "grp"),
        P("grp", None),
        P(),
    )
    out_specs = (P("seq", "grp"), P("seq", "grp"))
    return jax.shard_map(
        on_device, mesh=mesh, in_specs=in_specs, out_specs=out_specs, check_vma=False
    )
```

```python
import math

import jax
import jax.numpy as jnp
from jax import lax
from jax.experimental import pallas as pl
from jax.experimental.pallas import tpu as pltpu
from jax.sharding import PartitionSpec as P

HD = 128
ROWS = 320
WIDTH = 768
GROUP = 3 * HD
SHARE = GROUP // 4
SCALE = 1.4426950408889634 / math.sqrt(HD)
NEG = -1e30
NT = (((1,), (1,)), ((), ()))
PER_HEAD = 31


def sublayer_kernel(
    control_x,
    control,
    control_w,
    control_gate,
    base_x,
    base,
    base_w,
    base_gate,
    outs,
    kv,
    queries,
    best,
    accum,
    part_out,
    part_in,
    result,
    merged,
    w_control,
    w_base,
    proj,
    x_control,
    x_base,
    x_sem,
    q_sem,
    z_sem,
    far_sem,
    relay_sem,
    part_sem,
    o_sem,
    hand_sem,
    w_sem,
    local_sem,
    send_sem,
):
    grp = lax.axis_index("grp")
    seq = lax.axis_index("seq")
    half, core, y, z, x = grp // 2, grp % 2, seq // 16, (seq // 4) % 4, seq % 4
    here = (half, core, y, z, x)
    sibling = (half, 1 - core, y, z, x)
    above = (half, core, y, (z + 1) % 4, x)
    below = (half, core, y, (z + 3) % 4, x)
    right = (half, core, y, z, (x + 1) % 4)
    left = (half, core, y, z, (x + 3) % 4)
    across = (half, core, 1 - y, z, x)

    def ident(device):
        return {"grp": 2 * device[0] + device[1], "seq": 16 * device[2] + 4 * device[3] + device[4]}

    barrier = pltpu.get_barrier_semaphore()
    greeted = (
        [sibling, above, below, right, left, across, (half, core, y, z, (x + 2) % 4)]
        + [(half, x % 2, p, z, 2 * core + i) for i in range(2) for p in (y, 1 - y)]
        + [(half, z % 2, y, 2 * core + i, x) for i in range(2)]
        + [(f, x // 2, p, z, 2 * m + core) for f in range(2) for m in range(2) for p in (y, 1 - y)]
        + [(f, z // 2, y, 2 * m + core, x) for f in range(2) for m in range(2)]
        + [(1 - half, i, y, z, x) for i in range(2)]
    )
    for device in greeted:
        pl.semaphore_signal(barrier, inc=1, device_id=ident(device))

    lanes_out = pl.ds(pl.multiple_of(grp * WIDTH, WIDTH), WIDTH)
    locals_in = [
        pltpu.make_async_copy(control_w.at[:, :, lanes_out], w_control, local_sem.at[0]),
        pltpu.make_async_copy(base_w.at[:, lanes_out], w_base.at[grp], local_sem.at[1]),
        pltpu.make_async_copy(control_x.at[:, lanes_out], x_control, local_sem.at[2]),
        pltpu.make_async_copy(base_x, x_base, local_sem.at[3]),
    ]

    pl.semaphore_wait(barrier, len(greeted))

    def send(number, source, target, arrived, device, start, may_be_here=False):
        remote = pltpu.make_async_remote_copy(
            source, target, send_sem.at[number], arrived, device_id=ident(device)
        )
        act = remote.start if start else remote.wait_send
        if not may_be_here:
            act()
            return
        own = device[0] == here[0]
        for left, right in zip(device[1:], here[1:]):
            own = jnp.logical_and(own, left == right)
        pl.when(jnp.logical_not(own))(act)
        if start:

            @pl.when(own)
            def _():
                pltpu.make_async_copy(source, target, arrived).start()

    def arrive(ref, sem):
        pltpu.make_async_copy(ref, ref, sem).wait()

    def lanes(index):
        return pl.ds(pl.multiple_of(index * HD, HD), HD)

    def route(slot, m):
        if slot == 1:
            return 1, z % 2, (half, z // 2, y, 2 * m + core, x)
        plane = y if slot == 0 else 1 - y
        return 2 * plane, x % 2, (half, x // 2, plane, z, 2 * m + core)

    def pairs_out(slot, start):
        for m, ref, first in ((0, control, 3 * grp), (1, base, 0)):
            head, i, device = route(slot, m)
            send(
                PER_HEAD * slot + m,
                ref.at[pl.ds(1, 2), :, lanes(first + head)],
                kv.at[slot, :, 0, 0, i],
                x_sem.at[slot, i],
                device,
                start,
                True,
            )

    def queries_out(slot, start):
        for m, ref, first in ((0, control, 3 * grp), (1, base, 0)):
            head, i, device = route(slot, m)
            send(
                PER_HEAD * slot + 2 + m,
                ref.at[0, :, lanes(first + head)],
                queries.at[slot % 2, slot // 2, i],
                q_sem.at[slot % 2, slot // 2, i],
                device,
                start,
                True,
            )

    def ahead(h):
        return right if h == 1 else above

    def behind(h):
        return left if h == 1 else below

    def ring_out(h, i, start):
        block = kv.at[h, :, 0, 0, i]
        number = PER_HEAD * h + i
        send(number + 4, block, kv.at[h, :, 1, 0, i], z_sem.at[h, 0, i], ahead(h), start)
        send(number + 6, block, kv.at[h, :, 2, 0, i], z_sem.at[h, 1, i], behind(h), start)
        send(number + 8, block, kv.at[h, :, 0, 1, i], relay_sem.at[h, 0, i], sibling, start)

    def query_across(i, start):
        send(
            PER_HEAD + 10 + i,
            queries.at[1, 0, i],
            queries.at[1, 1, i],
            q_sem.at[1, 1, i],
            across,
            start,
        )

    def keys_on(h, i, start):
        number = PER_HEAD * h + i
        send(number + 12, kv.at[h, 0, 1, 0, i], kv.at[h, 0, 3, 0, i], far_sem.at[h, 0, i], ahead(h), start)
        block = kv.at[h, :, 1, 0, i]
        send(number + 16, block, kv.at[h, :, 1, 1, i], relay_sem.at[h, 1, i], sibling, start)

    def values_on(h, i, start):
        number = PER_HEAD * h + i
        send(number + 14, kv.at[h, 1, 2, 0, i], kv.at[h, 1, 3, 0, i], far_sem.at[h, 1, i], behind(h), start)
        block = kv.at[h, :, 2, 0, i]
        send(number + 18, block, kv.at[h, :, 2, 1, i], relay_sem.at[h, 2, i], sibling, start)

    def far_on(h, i, start):
        block = kv.at[h, :, 3, 0, i]
        send(PER_HEAD * h + 20 + i, block, kv.at[h, :, 3, 1, i], relay_sem.at[h, 3, i], sibling, start)

    def part_across(start):
        send(PER_HEAD + 22, part_out, part_in, part_sem.at[0], across, start)

    def home(slot, start):
        head, place = (1, z) if slot == 1 else (2 * y, x)
        for i in range(2):
            for f in range(2):
                if slot == 1:
                    owner = (f, z % 2, y, 2 * core + i, x)
                else:
                    owner = (f, x % 2, y if slot == 0 else 1 - y, z, 2 * core + i)
                send(
                    PER_HEAD * slot + 23 + 2 * i + f,
                    result.at[slot, i],
                    merged.at[head, place // 2, :, lanes(2 * half + place % 2)],
                    o_sem.at[head, place // 2, half],
                    owner,
                    start,
                    True,
                )

    def hand_over(h, m, f, start):
        block = merged.at[h, m, :, lanes(2 * f + core)]
        send(PER_HEAD * h + 27 + 2 * m + f, block, block, hand_sem.at[h, m, f], sibling, start)

    last = 3 * PER_HEAD
    share = pl.ds(pl.multiple_of(SHARE * x, SHARE), SHARE)

    def weights_beside(start):
        columns = pl.ds(pl.multiple_of((2 * half + 1 - core) * WIDTH, WIDTH), WIDTH)
        send(last, base_w.at[:, columns], w_base.at[grp], w_sem.at[0], sibling, start)

    def weights_across(start):
        for c in range(2):
            columns = pl.ds(pl.multiple_of((2 * (1 - half) + c) * WIDTH, WIDTH), WIDTH)
            send(
                last + 1 + c,
                base_w.at[share, columns],
                w_base.at[grp, share],
                w_sem.at[1 + core],
                (1 - half, c, y, z, x),
                start,
            )

    def weights_along(start):
        for d in range(1, 4):
            block = w_base.at[pl.ds(2 * (1 - half), 2), share]
            send(
                last + 2 + d, block, block, w_sem.at[2 + d], (half, core, y, z, (x + d) % 4), start
            )

    def order(h):
        place = z if h == 1 else x
        near = jnp.where(place // 2 == core, place % 2, 1 - place % 2)
        return near, 1 - near

    def blocks_in(h):
        for i in order(h):
            arrive(kv.at[h, :, 0, 0, i], x_sem.at[h, i])
            ring_out(h, i, True)

    def queries_in(group, side):
        for i in range(2):
            arrive(queries.at[group, side, i], q_sem.at[group, side, i])

    def neighbours_in(h):
        for i in order(h):
            arrive(kv.at[h, :, 1, 0, i], z_sem.at[h, 0, i])
            keys_on(h, i, True)
            arrive(kv.at[h, :, 2, 0, i], z_sem.at[h, 1, i])
            values_on(h, i, True)

    def far_in(h):
        for i in order(h):
            for j in range(2):
                arrive(kv.at[h, j, 3, 0, i], far_sem.at[h, j, i])
            far_on(h, i, True)

    def relayed(h, block):
        for i in range(2):
            arrive(kv.at[h, :, block, 1, i], relay_sem.at[h, block, i])

    def update(h, low, count, side=None):
        group = h % 2
        keys = kv[h, 0, low : low + count].reshape(count * 4 * ROWS, HD)
        values = kv[h, 1, low : low + count].reshape(count * 4 * ROWS, HD)
        values = jnp.concatenate([values, jnp.ones_like(values)], axis=1)
        if side is None:
            tiles = [(p, i, slice(0, ROWS)) for p in range(2) for i in range(2)]
        else:
            cut = ROWS // 2
            tiles = [(side, i, slice(k * cut, (k + 1) * cut)) for i in range(2) for k in range(2)]
        for p, i, rows in tiles:
            scores = lax.dot_general(
                queries[group, p, i, rows], keys, NT, preferred_element_type=jnp.float32
            )
            old = best[group, p, i, rows][:, :1]
            new = jnp.maximum(old, jnp.max(scores, axis=1, keepdims=True))
            weights = jnp.exp2(scores * SCALE - new * SCALE).astype(jnp.bfloat16)
            keep = jnp.exp2((old - new) * SCALE)
            best[group, p, i, rows] = jnp.broadcast_to(new, (new.shape[0], HD))
            accum[group, p, i, rows] = accum[group, p, i, rows] * keep + jnp.dot(
                weights, values, preferred_element_type=jnp.float32
            )

    lane = lax.broadcasted_iota(jnp.int32, (ROWS, HD), 1)

    def outcome(side, i):
        total = accum[1, side, i][:, HD:]
        return accum[1, side, i][:, :HD] / total, best[1, side, i] * SCALE + jnp.log2(total)

    def part():
        packed = jnp.zeros((ROWS, HD), jnp.float32)
        for i in range(2):
            value, rest = outcome(1, i)
            part_out[i] = value.astype(jnp.bfloat16)
            for j in range(3):
                piece = rest.astype(jnp.bfloat16).astype(jnp.float32)
                packed = jnp.where(lane == 3 * i + j, piece, packed)
                rest = rest - piece
        part_out[2] = packed.astype(jnp.bfloat16)
        part_across(True)

    def combine():
        arrive(part_in, part_sem.at[0])
        packed = part_in[2].astype(jnp.float32)
        for i in range(2):
            value, log_sum = outcome(0, i)
            other = (
                packed[:, 3 * i : 3 * i + 1]
                + packed[:, 3 * i + 1 : 3 * i + 2]
                + packed[:, 3 * i + 2 : 3 * i + 3]
            )
            top = jnp.maximum(log_sum, other)
            mine = jnp.exp2(log_sum - top)
            theirs = jnp.exp2(other - top)
            mixed = value * mine + part_in[i].astype(jnp.float32) * theirs
            result[1, i] = (mixed / (mine + theirs)).astype(jnp.bfloat16)
        home(1, True)

    def whole(slot):
        for i in range(2):
            done = accum[0, slot // 2, i]
            result[slot, i] = (done[:, :HD] / done[:, HD:]).astype(jnp.bfloat16)
        home(slot, True)

    def results_in(h):
        for m in range(2):
            for f in range(2):
                arrive(merged.at[h, m, :, lanes(2 * f + core)], o_sem.at[h, m, f])
                hand_over(h, m, f, True)

    def handed(h):
        for m in range(2):
            for f in range(2):
                arrive(merged.at[h, m, :, lanes(2 * f + 1 - core)], hand_sem.at[h, m, f])

    def term(h, m, columns):
        weight = (w_control, w_base)[m]
        rows = weight[:, lanes(h), columns].reshape(4 * HD, -1)
        return jnp.dot(merged[h, m], rows, preferred_element_type=jnp.float32)

    def project(h, first=False):
        handed(h)
        for m in range(2):
            new = term(h, m, slice(None))
            proj[m] = new if first else proj[m] + new

    pairs_out(0, True)
    pairs_out(1, True)
    queries_out(0, True)
    queries_out(2, True)
    queries_out(1, True)
    weights_across(True)
    pairs_out(2, True)
    weights_beside(True)
    for copy in locals_in:
        copy.start()
    best[...] = jnp.full(best.shape, NEG, jnp.float32)
    accum[...] = jnp.zeros(accum.shape, jnp.float32)
    blocks_in(0)
    blocks_in(1)
    queries_in(1, 0)
    for i in range(2):
        query_across(i, True)
    relayed(0, 0)
    queries_in(0, 0)
    queries_in(0, 1)
    update(0, 0, 1)
    blocks_in(2)
    neighbours_in(0)
    relayed(1, 0)
    queries_in(1, 1)
    update(1, 0, 1)
    neighbours_in(1)
    relayed(0, 1)
    relayed(0, 2)
    update(0, 1, 2)
    neighbours_in(2)
    far_in(0)
    far_in(1)
    for c in range(2):
        arrive(w_base.at[2 * (1 - half) + c, share], w_sem.at[1 + c])
    weights_along(True)
    relayed(0, 3)
    update(0, 3, 1)
    relayed(1, 1)
    relayed(1, 2)
    update(1, 1, 2)
    far_in(2)
    relayed(1, 3)
    update(1, 3, 1)
    part()
    relayed(2, 0)
    relayed(2, 1)
    update(2, 0, 2)
    combine()
    relayed(2, 2)
    relayed(2, 3)
    update(2, 2, 2, 1)
    whole(2)
    update(2, 2, 2, 0)
    whole(0)

    for h in range(3):
        pairs_out(h, False)
        queries_out(h, False)
        for i in range(2):
            ring_out(h, i, False)
            keys_on(h, i, False)
            values_on(h, i, False)
            far_on(h, i, False)
    for i in range(2):
        query_across(i, False)
    part_across(False)
    weights_beside(False)
    weights_across(False)
    weights_along(False)
    for copy in locals_in:
        copy.wait()
    arrive(w_base.at[2 * half + 1 - core], w_sem.at[0])
    for d in range(1, 4):
        rows = pl.ds(pl.multiple_of(SHARE * ((x + 4 - d) % 4), SHARE), SHARE)
        arrive(w_base.at[pl.ds(2 * (1 - half), 2), rows], w_sem.at[2 + d])
    results_in(1)
    project(1, True)
    results_in(2 * (1 - y))
    project(2 * (1 - y))
    results_in(2 * y)
    handed(2 * y)
    per_row = WIDTH // HD
    for k in range(3):
        columns = slice(2 * k * HD, (2 * k + 2) * HD)
        gates = [
            jnp.concatenate([gate[pl.ds(grp * per_row + 2 * k + j, 1), :] for j in range(2)], axis=1)
            for gate in (control_gate, base_gate)
        ]
        sums = [proj[m, :, columns] + term(2 * y, m, columns) for m in range(2)]
        first = (x_control[:, columns].astype(jnp.float32) + gates[0] * sums[0]).astype(jnp.bfloat16)
        outs[0, :, columns] = first
        second = x_base[:, columns].astype(jnp.float32) + gates[1] * sums[1]
        outs[1, :, columns] = (second + first.astype(jnp.float32)).astype(jnp.bfloat16)

    for h in range(3):
        home(h, False)
        for m in range(2):
            for f in range(2):
                hand_over(h, m, f, False)


def on_device(
    control_x, control_qkv, control_out_w, control_gate, base_x, base_qkv, base_out_w, base_gate
):
    vmem = pl.BlockSpec(memory_space=pltpu.VMEM)
    anywhere = pl.BlockSpec(memory_space=pl.ANY)
    dma = pltpu.SemaphoreType.DMA
    half16 = jnp.bfloat16
    full32 = jnp.float32
    outs = pl.pallas_call(
        sublayer_kernel,
        out_shape=jax.ShapeDtypeStruct((2, ROWS, WIDTH), half16),
        in_specs=[anywhere, anywhere, anywhere, vmem, anywhere, anywhere, anywhere, vmem],
        out_specs=vmem,
        scratch_shapes=[
            pltpu.VMEM((3, 2, 4, 2, 2, ROWS, HD), half16),
            pltpu.VMEM((2, 2, 2, ROWS, HD), half16),
            pltpu.VMEM((2, 2, 2, ROWS, HD), full32),
            pltpu.VMEM((2, 2, 2, ROWS, 2 * HD), full32),
            pltpu.VMEM((3, ROWS, HD), half16),
            pltpu.VMEM((3, ROWS, HD), half16),
            pltpu.VMEM((3, 2, ROWS, HD), half16),
            pltpu.VMEM((3, 2, ROWS, 4 * HD), half16),
            pltpu.VMEM((4, GROUP, WIDTH), half16),
            pltpu.VMEM((4, GROUP, WIDTH), half16),
            pltpu.VMEM((2, ROWS, WIDTH), full32),
            pltpu.VMEM((ROWS, WIDTH), half16),
            pltpu.VMEM((ROWS, WIDTH), half16),
            dma((3, 2)),
            dma((2, 2, 2)),
            dma((3, 2, 2)),
            dma((3, 2, 2)),
            dma((3, 4, 2)),
            dma((1,)),
            dma((3, 2, 2)),
            dma((3, 2, 2)),
            dma((6,)),
            dma((4,)),
            dma((3 * PER_HEAD + 6,)),
        ],
        compiler_params=pltpu.CompilerParams(
            collective_id=0, has_side_effects=True, vmem_limit_bytes=60 * 2**20
        ),
        name="sublayer",
    )(
        control_x,
        control_qkv.transpose(1, 0, 2),
        control_out_w.reshape(4, GROUP, 4 * WIDTH),
        control_gate.reshape(4 * WIDTH // HD, HD),
        base_x,
        base_qkv.transpose(1, 0, 2),
        base_out_w,
        base_gate.reshape(4 * WIDTH // HD, HD),
    )
    return outs[0], outs[1]


def solution(mesh):
    in_specs = (
        P("seq", None),
        P("seq", None, None),
        P(),
        P(),
        P("seq", "grp"),
        P("seq", None, "grp"),
        P("grp", None),
        P(),
    )
    out_specs = (P("seq", "grp"), P("seq", "grp"))
    return jax.shard_map(
        on_device, mesh=mesh, in_specs=in_specs, out_specs=out_specs, check_vma=False
    )
```

```python
import math

import jax
import jax.numpy as jnp
from jax import lax
from jax.experimental import pallas as pl
from jax.experimental.pallas import tpu as pltpu
from jax.sharding import PartitionSpec as P

HD = 128
ROWS = 320
WIDTH = 768
GROUP = 3 * HD
SHARE = GROUP // 4
SCALE = 1.4426950408889634 / math.sqrt(HD)
NEG = -1e30
NT = (((1,), (1,)), ((), ()))
PER_HEAD = 31


def sublayer_kernel(
    control_x,
    control,
    control_w,
    control_gate,
    base_x,
    base,
    base_w,
    base_gate,
    outs,
    kv,
    queries,
    best,
    accum,
    part_out,
    part_in,
    result,
    merged,
    w_control,
    w_base,
    proj,
    x_control,
    x_base,
    x_sem,
    q_sem,
    z_sem,
    far_sem,
    relay_sem,
    part_sem,
    o_sem,
    hand_sem,
    w_sem,
    local_sem,
    send_sem,
):
    grp = lax.axis_index("grp")
    seq = lax.axis_index("seq")
    half, core, y, z, x = grp // 2, grp % 2, seq // 16, (seq // 4) % 4, seq % 4
    here = (half, core, y, z, x)
    sibling = (half, 1 - core, y, z, x)
    above = (half, core, y, (z + 1) % 4, x)
    below = (half, core, y, (z + 3) % 4, x)
    right = (half, core, y, z, (x + 1) % 4)
    left = (half, core, y, z, (x + 3) % 4)
    across = (half, core, 1 - y, z, x)

    def ident(device):
        return {"grp": 2 * device[0] + device[1], "seq": 16 * device[2] + 4 * device[3] + device[4]}

    barrier = pltpu.get_barrier_semaphore()
    greeted = (
        [sibling, above, below, right, left, across, (half, core, y, z, (x + 2) % 4)]
        + [(half, x % 2, p, z, 2 * core + i) for i in range(2) for p in (y, 1 - y)]
        + [(half, z % 2, y, 2 * core + i, x) for i in range(2)]
        + [(f, x // 2, p, z, 2 * m + core) for f in range(2) for m in range(2) for p in (y, 1 - y)]
        + [(f, z // 2, y, 2 * m + core, x) for f in range(2) for m in range(2)]
        + [(1 - half, i, y, z, x) for i in range(2)]
    )
    for device in greeted:
        pl.semaphore_signal(barrier, inc=1, device_id=ident(device))

    lanes_out = pl.ds(pl.multiple_of(grp * WIDTH, WIDTH), WIDTH)
    locals_in = [
        pltpu.make_async_copy(control_w.at[:, :, lanes_out], w_control, local_sem.at[0]),
        pltpu.make_async_copy(base_w.at[:, lanes_out], w_base.at[grp], local_sem.at[1]),
        pltpu.make_async_copy(control_x.at[:, lanes_out], x_control, local_sem.at[2]),
        pltpu.make_async_copy(base_x, x_base, local_sem.at[3]),
    ]

    pl.semaphore_wait(barrier, len(greeted))

    def send(number, source, target, arrived, device, start, may_be_here=False):
        remote = pltpu.make_async_remote_copy(
            source, target, send_sem.at[number], arrived, device_id=ident(device)
        )
        act = remote.start if start else remote.wait_send
        if not may_be_here:
            act()
            return
        own = device[0] == here[0]
        for left, right in zip(device[1:], here[1:]):
            own = jnp.logical_and(own, left == right)
        pl.when(jnp.logical_not(own))(act)
        if start:

            @pl.when(own)
            def _():
                pltpu.make_async_copy(source, target, arrived).start()

    def arrive(ref, sem):
        pltpu.make_async_copy(ref, ref, sem).wait()

    def lanes(index):
        return pl.ds(pl.multiple_of(index * HD, HD), HD)

    def route(slot, m):
        if slot == 1:
            return 1, z % 2, (half, z // 2, y, 2 * m + core, x)
        plane = y if slot == 0 else 1 - y
        return 2 * plane, x % 2, (half, x // 2, plane, z, 2 * m + core)

    def pairs_out(slot, start):
        for m, ref, first in ((0, control, 3 * grp), (1, base, 0)):
            head, i, device = route(slot, m)
            send(
                PER_HEAD * slot + m,
                ref.at[pl.ds(1, 2), :, lanes(first + head)],
                kv.at[slot, :, 0, 0, i],
                x_sem.at[slot, i],
                device,
                start,
                True,
            )

    def queries_out(slot, start):
        for m, ref, first in ((0, control, 3 * grp), (1, base, 0)):
            head, i, device = route(slot, m)
            send(
                PER_HEAD * slot + 2 + m,
                ref.at[0, :, lanes(first + head)],
                queries.at[slot % 2, slot // 2, i],
                q_sem.at[slot % 2, slot // 2, i],
                device,
                start,
                True,
            )

    def ahead(h):
        return right if h == 1 else above

    def behind(h):
        return left if h == 1 else below

    def ring_out(h, i, start):
        block = kv.at[h, :, 0, 0, i]
        number = PER_HEAD * h + i
        send(number + 4, block, kv.at[h, :, 1, 0, i], z_sem.at[h, 0, i], ahead(h), start)
        send(number + 6, block, kv.at[h, :, 2, 0, i], z_sem.at[h, 1, i], behind(h), start)
        send(number + 8, block, kv.at[h, :, 0, 1, i], relay_sem.at[h, 0, i], sibling, start)

    def query_across(i, start):
        send(
            PER_HEAD + 10 + i,
            queries.at[1, 0, i],
            queries.at[1, 1, i],
            q_sem.at[1, 1, i],
            across,
            start,
        )

    def keys_on(h, i, start):
        number = PER_HEAD * h + i
        send(number + 12, kv.at[h, 0, 1, 0, i], kv.at[h, 0, 3, 0, i], far_sem.at[h, 0, i], ahead(h), start)
        block = kv.at[h, :, 1, 0, i]
        send(number + 16, block, kv.at[h, :, 1, 1, i], relay_sem.at[h, 1, i], sibling, start)

    def values_on(h, i, start):
        number = PER_HEAD * h + i
        send(number + 14, kv.at[h, 1, 2, 0, i], kv.at[h, 1, 3, 0, i], far_sem.at[h, 1, i], behind(h), start)
        block = kv.at[h, :, 2, 0, i]
        send(number + 18, block, kv.at[h, :, 2, 1, i], relay_sem.at[h, 2, i], sibling, start)

    def far_on(h, i, start):
        block = kv.at[h, :, 3, 0, i]
        send(PER_HEAD * h + 20 + i, block, kv.at[h, :, 3, 1, i], relay_sem.at[h, 3, i], sibling, start)

    def part_across(start):
        send(PER_HEAD + 22, part_out, part_in, part_sem.at[0], across, start)

    def home(slot, start):
        head, place = (1, z) if slot == 1 else (2 * y, x)
        for i in range(2):
            for f in range(2):
                if slot == 1:
                    owner = (f, z % 2, y, 2 * core + i, x)
                else:
                    owner = (f, x % 2, y if slot == 0 else 1 - y, z, 2 * core + i)
                send(
                    PER_HEAD * slot + 23 + 2 * i + f,
                    result.at[slot, i],
                    merged.at[head, place // 2, :, lanes(2 * half + place % 2)],
                    o_sem.at[head, place // 2, half],
                    owner,
                    start,
                    True,
                )

    def hand_over(h, m, f, start):
        block = merged.at[h, m, :, lanes(2 * f + core)]
        send(PER_HEAD * h + 27 + 2 * m + f, block, block, hand_sem.at[h, m, f], sibling, start)

    last = 3 * PER_HEAD
    share = pl.ds(pl.multiple_of(SHARE * x, SHARE), SHARE)

    def weights_beside(start):
        columns = pl.ds(pl.multiple_of((2 * half + 1 - core) * WIDTH, WIDTH), WIDTH)
        send(last, base_w.at[:, columns], w_base.at[grp], w_sem.at[0], sibling, start)

    def weights_across(start):
        for c in range(2):
            columns = pl.ds(pl.multiple_of((2 * (1 - half) + c) * WIDTH, WIDTH), WIDTH)
            send(
                last + 1 + c,
                base_w.at[share, columns],
                w_base.at[grp, share],
                w_sem.at[1 + core],
                (1 - half, c, y, z, x),
                start,
            )

    def weights_along(start):
        for d in range(1, 4):
            block = w_base.at[pl.ds(2 * (1 - half), 2), share]
            send(
                last + 2 + d, block, block, w_sem.at[2 + d], (half, core, y, z, (x + d) % 4), start
            )

    def order(h):
        place = z if h == 1 else x
        near = jnp.where(place // 2 == core, place % 2, 1 - place % 2)
        return near, 1 - near

    def blocks_in(h):
        for i in order(h):
            arrive(kv.at[h, :, 0, 0, i], x_sem.at[h, i])
            ring_out(h, i, True)

    def queries_in(group, side):
        for i in range(2):
            arrive(queries.at[group, side, i], q_sem.at[group, side, i])

    def neighbours_in(h):
        for i in order(h):
            arrive(kv.at[h, :, 1, 0, i], z_sem.at[h, 0, i])
            keys_on(h, i, True)
            arrive(kv.at[h, :, 2, 0, i], z_sem.at[h, 1, i])
            values_on(h, i, True)

    def far_in(h):
        for i in order(h):
            for j in range(2):
                arrive(kv.at[h, j, 3, 0, i], far_sem.at[h, j, i])
            far_on(h, i, True)

    def relayed(h, block):
        for i in range(2):
            arrive(kv.at[h, :, block, 1, i], relay_sem.at[h, block, i])

    def update(h, block):
        group = h % 2
        keys = kv[h, 0, block].reshape(4 * ROWS, HD)
        values = kv[h, 1, block].reshape(4 * ROWS, HD)
        values = jnp.concatenate([values, jnp.ones_like(values)], axis=1)
        for p in range(2):
            for i in range(2):
                scores = lax.dot_general(
                    queries[group, p, i], keys, NT, preferred_element_type=jnp.float32
                )
                old = best[group, p, i][:, :1]
                new = jnp.maximum(old, jnp.max(scores, axis=1, keepdims=True))
                weights = jnp.exp2(scores * SCALE - new * SCALE).astype(jnp.bfloat16)
                keep = jnp.exp2((old - new) * SCALE)
                best[group, p, i] = jnp.broadcast_to(new, (ROWS, HD))
                accum[group, p, i] = accum[group, p, i] * keep + jnp.dot(
                    weights, values, preferred_element_type=jnp.float32
                )

    lane = lax.broadcasted_iota(jnp.int32, (ROWS, HD), 1)

    def outcome(side, i):
        total = accum[1, side, i][:, HD:]
        return accum[1, side, i][:, :HD] / total, best[1, side, i] * SCALE + jnp.log2(total)

    def part():
        packed = jnp.zeros((ROWS, HD), jnp.float32)
        for i in range(2):
            value, rest = outcome(1, i)
            part_out[i] = value.astype(jnp.bfloat16)
            for j in range(3):
                piece = rest.astype(jnp.bfloat16).astype(jnp.float32)
                packed = jnp.where(lane == 3 * i + j, piece, packed)
                rest = rest - piece
        part_out[2] = packed.astype(jnp.bfloat16)
        part_across(True)

    def combine():
        arrive(part_in, part_sem.at[0])
        packed = part_in[2].astype(jnp.float32)
        for i in range(2):
            value, log_sum = outcome(0, i)
            other = (
                packed[:, 3 * i : 3 * i + 1]
                + packed[:, 3 * i + 1 : 3 * i + 2]
                + packed[:, 3 * i + 2 : 3 * i + 3]
            )
            top = jnp.maximum(log_sum, other)
            mine = jnp.exp2(log_sum - top)
            theirs = jnp.exp2(other - top)
            mixed = value * mine + part_in[i].astype(jnp.float32) * theirs
            result[1, i] = (mixed / (mine + theirs)).astype(jnp.bfloat16)
        home(1, True)

    def whole(slot):
        for i in range(2):
            done = accum[0, slot // 2, i]
            result[slot, i] = (done[:, :HD] / done[:, HD:]).astype(jnp.bfloat16)
        home(slot, True)

    def results_in(h):
        for m in range(2):
            for f in range(2):
                arrive(merged.at[h, m, :, lanes(2 * f + core)], o_sem.at[h, m, f])
                hand_over(h, m, f, True)

    def handed(h):
        for m in range(2):
            for f in range(2):
                arrive(merged.at[h, m, :, lanes(2 * f + 1 - core)], hand_sem.at[h, m, f])

    def term(h, m, columns):
        weight = (w_control, w_base)[m]
        rows = weight[:, lanes(h), columns].reshape(4 * HD, -1)
        return jnp.dot(merged[h, m], rows, preferred_element_type=jnp.float32)

    def project(h, first=False):
        handed(h)
        for m in range(2):
            new = term(h, m, slice(None))
            proj[m] = new if first else proj[m] + new

    pairs_out(0, True)
    pairs_out(1, True)
    queries_out(0, True)
    queries_out(2, True)
    queries_out(1, True)
    weights_across(True)
    pairs_out(2, True)
    weights_beside(True)
    for copy in locals_in:
        copy.start()
    best[...] = jnp.full(best.shape, NEG, jnp.float32)
    accum[...] = jnp.zeros(accum.shape, jnp.float32)
    blocks_in(0)
    blocks_in(1)
    queries_in(1, 0)
    for i in range(2):
        query_across(i, True)
    queries_in(0, 0)
    queries_in(0, 1)

    steps = (
        (0, 0), (1, 0), (0, 1), (0, 2), (1, 1), (0, 3), (1, 2), (1, 3), (2, 0), (2, 1), (2, 2), (2, 3)
    )

    def pick(t, which):
        found = jnp.int32(steps[0][which])
        for k, entry in enumerate(steps):
            found = jnp.where(t == k, entry[which], found)
        return found

    def step(t, carry):
        slot, block = pick(t, 0), pick(t, 1)

        @pl.when(t == 1)
        def _():
            blocks_in(2)
            neighbours_in(0)
            queries_in(1, 1)

        @pl.when(t == 2)
        def _():
            neighbours_in(1)

        @pl.when(t == 4)
        def _():
            neighbours_in(2)
            far_in(0)

        @pl.when(t == 5)
        def _():
            far_in(1)
            for c in range(2):
                arrive(w_base.at[2 * (1 - half) + c, share], w_sem.at[1 + c])
            weights_along(True)

        @pl.when(t == 7)
        def _():
            far_in(2)

        @pl.when(t == 8)
        def _():
            part()

        @pl.when(t == 10)
        def _():
            combine()

        relayed(slot, block)
        update(slot, block)
        return carry

    lax.fori_loop(0, len(steps), step, 0)
    whole(2)
    whole(0)

    for h in range(3):
        pairs_out(h, False)
        queries_out(h, False)
        for i in range(2):
            ring_out(h, i, False)
            keys_on(h, i, False)
            values_on(h, i, False)
            far_on(h, i, False)
    for i in range(2):
        query_across(i, False)
    part_across(False)
    weights_beside(False)
    weights_across(False)
    weights_along(False)
    for copy in locals_in:
        copy.wait()
    arrive(w_base.at[2 * half + 1 - core], w_sem.at[0])
    for d in range(1, 4):
        rows = pl.ds(pl.multiple_of(SHARE * ((x + 4 - d) % 4), SHARE), SHARE)
        arrive(w_base.at[pl.ds(2 * (1 - half), 2), rows], w_sem.at[2 + d])
    results_in(1)
    project(1, True)
    results_in(2 * (1 - y))
    project(2 * (1 - y))
    results_in(2 * y)
    handed(2 * y)
    per_row = WIDTH // HD
    for k in range(3):
        columns = slice(2 * k * HD, (2 * k + 2) * HD)
        gates = [
            jnp.concatenate([gate[pl.ds(grp * per_row + 2 * k + j, 1), :] for j in range(2)], axis=1)
            for gate in (control_gate, base_gate)
        ]
        sums = [proj[m, :, columns] + term(2 * y, m, columns) for m in range(2)]
        first = (x_control[:, columns].astype(jnp.float32) + gates[0] * sums[0]).astype(jnp.bfloat16)
        outs[0, :, columns] = first
        second = x_base[:, columns].astype(jnp.float32) + gates[1] * sums[1]
        outs[1, :, columns] = (second + first.astype(jnp.float32)).astype(jnp.bfloat16)

    for h in range(3):
        home(h, False)
        for m in range(2):
            for f in range(2):
                hand_over(h, m, f, False)


def on_device(
    control_x, control_qkv, control_out_w, control_gate, base_x, base_qkv, base_out_w, base_gate
):
    vmem = pl.BlockSpec(memory_space=pltpu.VMEM)
    anywhere = pl.BlockSpec(memory_space=pl.ANY)
    dma = pltpu.SemaphoreType.DMA
    half16 = jnp.bfloat16
    full32 = jnp.float32
    outs = pl.pallas_call(
        sublayer_kernel,
        out_shape=jax.ShapeDtypeStruct((2, ROWS, WIDTH), half16),
        in_specs=[anywhere, anywhere, anywhere, vmem, anywhere, anywhere, anywhere, vmem],
        out_specs=vmem,
        scratch_shapes=[
            pltpu.VMEM((3, 2, 4, 2, 2, ROWS, HD), half16),
            pltpu.VMEM((2, 2, 2, ROWS, HD), half16),
            pltpu.VMEM((2, 2, 2, ROWS, HD), full32),
            pltpu.VMEM((2, 2, 2, ROWS, 2 * HD), full32),
            pltpu.VMEM((3, ROWS, HD), half16),
            pltpu.VMEM((3, ROWS, HD), half16),
            pltpu.VMEM((3, 2, ROWS, HD), half16),
            pltpu.VMEM((3, 2, ROWS, 4 * HD), half16),
            pltpu.VMEM((4, GROUP, WIDTH), half16),
            pltpu.VMEM((4, GROUP, WIDTH), half16),
            pltpu.VMEM((2, ROWS, WIDTH), full32),
            pltpu.VMEM((ROWS, WIDTH), half16),
            pltpu.VMEM((ROWS, WIDTH), half16),
            dma((3, 2)),
            dma((2, 2, 2)),
            dma((3, 2, 2)),
            dma((3, 2, 2)),
            dma((3, 4, 2)),
            dma((1,)),
            dma((3, 2, 2)),
            dma((3, 2, 2)),
            dma((6,)),
            dma((4,)),
            dma((3 * PER_HEAD + 6,)),
        ],
        compiler_params=pltpu.CompilerParams(
            collective_id=0, has_side_effects=True, vmem_limit_bytes=60 * 2**20
        ),
        name="sublayer",
    )(
        control_x,
        control_qkv.transpose(1, 0, 2),
        control_out_w.reshape(4, GROUP, 4 * WIDTH),
        control_gate.reshape(4 * WIDTH // HD, HD),
        base_x,
        base_qkv.transpose(1, 0, 2),
        base_out_w,
        base_gate.reshape(4 * WIDTH // HD, HD),
    )
    return outs[0], outs[1]


def solution(mesh):
    in_specs = (
        P("seq", None),
        P("seq", None, None),
        P(),
        P(),
        P("seq", "grp"),
        P("seq", None, "grp"),
        P("grp", None),
        P(),
    )
    out_specs = (P("seq", "grp"), P("seq", "grp"))
    return jax.shard_map(
        on_device, mesh=mesh, in_specs=in_specs, out_specs=out_specs, check_vma=False
    )
```

```python
import math

import jax
import jax.numpy as jnp
from jax import lax
from jax.experimental import pallas as pl
from jax.experimental.pallas import tpu as pltpu
from jax.sharding import PartitionSpec as P

HD = 128
ROWS = 320
WIDTH = 768
GROUP = 3 * HD
SHARE = GROUP // 4
SCALE = 1.4426950408889634 / math.sqrt(HD)
NEG = -1e30
NT = (((1,), (1,)), ((), ()))
PER_HEAD = 31


def sublayer_kernel(
    control_x,
    control,
    control_w,
    control_gate,
    base_x,
    base,
    base_w,
    base_gate,
    outs,
    kv,
    queries,
    best,
    accum,
    part_out,
    part_in,
    result,
    merged,
    w_control,
    w_base,
    proj,
    x_control,
    x_base,
    x_sem,
    q_sem,
    z_sem,
    far_sem,
    relay_sem,
    part_sem,
    o_sem,
    hand_sem,
    w_sem,
    local_sem,
    send_sem,
):
    grp = lax.axis_index("grp")
    seq = lax.axis_index("seq")
    half, core, y, z, x = grp // 2, grp % 2, seq // 16, (seq // 4) % 4, seq % 4
    here = (half, core, y, z, x)
    sibling = (half, 1 - core, y, z, x)
    above = (half, core, y, (z + 1) % 4, x)
    below = (half, core, y, (z + 3) % 4, x)
    right = (half, core, y, z, (x + 1) % 4)
    left = (half, core, y, z, (x + 3) % 4)
    across = (half, core, 1 - y, z, x)

    def ident(device):
        return {"grp": 2 * device[0] + device[1], "seq": 16 * device[2] + 4 * device[3] + device[4]}

    barrier = pltpu.get_barrier_semaphore()
    greeted = (
        [sibling, above, below, right, left, across, (half, core, y, z, (x + 2) % 4)]
        + [(half, x % 2, p, z, 2 * core + i) for i in range(2) for p in (y, 1 - y)]
        + [(half, z % 2, y, 2 * core + i, x) for i in range(2)]
        + [(f, x // 2, p, z, 2 * m + core) for f in range(2) for m in range(2) for p in (y, 1 - y)]
        + [(f, z // 2, y, 2 * m + core, x) for f in range(2) for m in range(2)]
        + [(1 - half, i, y, z, x) for i in range(2)]
    )
    for device in greeted:
        pl.semaphore_signal(barrier, inc=1, device_id=ident(device))

    lanes_out = pl.ds(pl.multiple_of(grp * WIDTH, WIDTH), WIDTH)
    locals_in = [
        pltpu.make_async_copy(control_w.at[:, :, lanes_out], w_control, local_sem.at[0]),
        pltpu.make_async_copy(base_w.at[:, lanes_out], w_base.at[grp], local_sem.at[1]),
        pltpu.make_async_copy(control_x.at[:, lanes_out], x_control, local_sem.at[2]),
        pltpu.make_async_copy(base_x, x_base, local_sem.at[3]),
    ]

    pl.semaphore_wait(barrier, len(greeted))

    def send(number, source, target, arrived, device, start, may_be_here=False):
        remote = pltpu.make_async_remote_copy(
            source, target, send_sem.at[number], arrived, device_id=ident(device)
        )
        act = remote.start if start else remote.wait_send
        if not may_be_here:
            act()
            return
        own = device[0] == here[0]
        for left, right in zip(device[1:], here[1:]):
            own = jnp.logical_and(own, left == right)
        pl.when(jnp.logical_not(own))(act)
        if start:

            @pl.when(own)
            def _():
                pltpu.make_async_copy(source, target, arrived).start()

    def arrive(ref, sem):
        pltpu.make_async_copy(ref, ref, sem).wait()

    def lanes(index):
        return pl.ds(pl.multiple_of(index * HD, HD), HD)

    def route(slot, m):
        if slot == 1:
            return 1, z % 2, (half, z // 2, y, 2 * m + core, x)
        plane = y if slot == 0 else 1 - y
        return 2 * plane, x % 2, (half, x // 2, plane, z, 2 * m + core)

    def pairs_out(slot, start):
        for m, ref, first in ((0, control, 3 * grp), (1, base, 0)):
            head, i, device = route(slot, m)
            send(
                PER_HEAD * slot + m,
                ref.at[pl.ds(1, 2), :, lanes(first + head)],
                kv.at[slot, :, 0, 0, i],
                x_sem.at[slot, i],
                device,
                start,
                True,
            )

    def queries_out(slot, start):
        for m, ref, first in ((0, control, 3 * grp), (1, base, 0)):
            head, i, device = route(slot, m)
            send(
                PER_HEAD * slot + 2 + m,
                ref.at[0, :, lanes(first + head)],
                queries.at[slot % 2, slot // 2, i],
                q_sem.at[slot % 2, slot // 2, i],
                device,
                start,
                True,
            )

    def ahead(h):
        return right if h == 1 else above

    def behind(h):
        return left if h == 1 else below

    def ring_out(h, i, start):
        block = kv.at[h, :, 0, 0, i]
        number = PER_HEAD * h + i
        send(number + 4, block, kv.at[h, :, 1, 0, i], z_sem.at[h, 0, i], ahead(h), start)
        send(number + 6, block, kv.at[h, :, 2, 0, i], z_sem.at[h, 1, i], behind(h), start)
        send(number + 8, block, kv.at[h, :, 0, 1, i], relay_sem.at[h, 0, i], sibling, start)

    def query_across(i, start):
        send(
            PER_HEAD + 10 + i,
            queries.at[1, 0, i],
            queries.at[1, 1, i],
            q_sem.at[1, 1, i],
            across,
            start,
        )

    def keys_on(h, i, start):
        number = PER_HEAD * h + i
        send(number + 12, kv.at[h, 0, 1, 0, i], kv.at[h, 0, 3, 0, i], far_sem.at[h, 0, i], ahead(h), start)
        block = kv.at[h, :, 1, 0, i]
        send(number + 16, block, kv.at[h, :, 1, 1, i], relay_sem.at[h, 1, i], sibling, start)

    def values_on(h, i, start):
        number = PER_HEAD * h + i
        send(number + 14, kv.at[h, 1, 2, 0, i], kv.at[h, 1, 3, 0, i], far_sem.at[h, 1, i], behind(h), start)
        block = kv.at[h, :, 2, 0, i]
        send(number + 18, block, kv.at[h, :, 2, 1, i], relay_sem.at[h, 2, i], sibling, start)

    def far_on(h, i, start):
        block = kv.at[h, :, 3, 0, i]
        send(PER_HEAD * h + 20 + i, block, kv.at[h, :, 3, 1, i], relay_sem.at[h, 3, i], sibling, start)

    def part_across(start):
        send(PER_HEAD + 22, part_out, part_in, part_sem.at[0], across, start)

    def home(slot, start):
        head, place = (1, z) if slot == 1 else (2 * y, x)
        for i in range(2):
            for f in range(2):
                if slot == 1:
                    owner = (f, z % 2, y, 2 * core + i, x)
                else:
                    owner = (f, x % 2, y if slot == 0 else 1 - y, z, 2 * core + i)
                send(
                    PER_HEAD * slot + 23 + 2 * i + f,
                    result.at[slot, i],
                    merged.at[head, place // 2, :, lanes(2 * half + place % 2)],
                    o_sem.at[head, place // 2, half],
                    owner,
                    start,
                    True,
                )

    def hand_over(h, m, f, start):
        block = merged.at[h, m, :, lanes(2 * f + core)]
        send(PER_HEAD * h + 27 + 2 * m + f, block, block, hand_sem.at[h, m, f], sibling, start)

    last = 3 * PER_HEAD
    share = pl.ds(pl.multiple_of(SHARE * x, SHARE), SHARE)

    def weights_beside(start):
        columns = pl.ds(pl.multiple_of((2 * half + 1 - core) * WIDTH, WIDTH), WIDTH)
        send(last, base_w.at[:, columns], w_base.at[grp], w_sem.at[0], sibling, start)

    def weights_across(start):
        for c in range(2):
            columns = pl.ds(pl.multiple_of((2 * (1 - half) + c) * WIDTH, WIDTH), WIDTH)
            send(
                last + 1 + c,
                base_w.at[share, columns],
                w_base.at[grp, share],
                w_sem.at[1 + core],
                (1 - half, c, y, z, x),
                start,
            )

    def weights_along(start):
        for d in range(1, 4):
            block = w_base.at[pl.ds(2 * (1 - half), 2), share]
            send(
                last + 2 + d, block, block, w_sem.at[2 + d], (half, core, y, z, (x + d) % 4), start
            )

    def order(h):
        place = z if h == 1 else x
        near = jnp.where(place // 2 == core, place % 2, 1 - place % 2)
        return near, 1 - near

    def blocks_in(h):
        for i in order(h):
            arrive(kv.at[h, :, 0, 0, i], x_sem.at[h, i])
            ring_out(h, i, True)

    def queries_in(group, side):
        for i in range(2):
            arrive(queries.at[group, side, i], q_sem.at[group, side, i])

    def neighbours_in(h):
        for i in order(h):
            arrive(kv.at[h, :, 1, 0, i], z_sem.at[h, 0, i])
            keys_on(h, i, True)
            arrive(kv.at[h, :, 2, 0, i], z_sem.at[h, 1, i])
            values_on(h, i, True)

    def far_in(h):
        for i in order(h):
            for j in range(2):
                arrive(kv.at[h, j, 3, 0, i], far_sem.at[h, j, i])
            far_on(h, i, True)

    def relayed(h, block):
        for i in range(2):
            arrive(kv.at[h, :, block, 1, i], relay_sem.at[h, block, i])

    def update(tiles, h, low, count):
        group = h % 2
        keys = kv[h, 0, pl.ds(low, count)].reshape(count * 4 * ROWS, HD)
        values = kv[h, 1, pl.ds(low, count)].reshape(count * 4 * ROWS, HD)
        values = jnp.concatenate([values, jnp.ones_like(values)], axis=1)
        for p, i, rows in tiles:
            scores = lax.dot_general(
                queries[group, p, i, rows], keys, NT, preferred_element_type=jnp.float32
            )
            old = best[group, p, i, rows][:, :1]
            new = jnp.maximum(old, jnp.max(scores, axis=1, keepdims=True))
            weights = jnp.exp2(scores * SCALE - new * SCALE).astype(jnp.bfloat16)
            keep = jnp.exp2((old - new) * SCALE)
            best[group, p, i, rows] = jnp.broadcast_to(new, (new.shape[0], HD))
            accum[group, p, i, rows] = accum[group, p, i, rows] * keep + jnp.dot(
                weights, values, preferred_element_type=jnp.float32
            )

    lane = lax.broadcasted_iota(jnp.int32, (ROWS, HD), 1)

    def outcome(side, i):
        total = accum[1, side, i][:, HD:]
        return accum[1, side, i][:, :HD] / total, best[1, side, i] * SCALE + jnp.log2(total)

    def part():
        packed = jnp.zeros((ROWS, HD), jnp.float32)
        for i in range(2):
            value, rest = outcome(1, i)
            part_out[i] = value.astype(jnp.bfloat16)
            for j in range(3):
                piece = rest.astype(jnp.bfloat16).astype(jnp.float32)
                packed = jnp.where(lane == 3 * i + j, piece, packed)
                rest = rest - piece
        part_out[2] = packed.astype(jnp.bfloat16)
        part_across(True)

    def combine():
        arrive(part_in, part_sem.at[0])
        packed = part_in[2].astype(jnp.float32)
        for i in range(2):
            value, log_sum = outcome(0, i)
            other = (
                packed[:, 3 * i : 3 * i + 1]
                + packed[:, 3 * i + 1 : 3 * i + 2]
                + packed[:, 3 * i + 2 : 3 * i + 3]
            )
            top = jnp.maximum(log_sum, other)
            mine = jnp.exp2(log_sum - top)
            theirs = jnp.exp2(other - top)
            mixed = value * mine + part_in[i].astype(jnp.float32) * theirs
            result[1, i] = (mixed / (mine + theirs)).astype(jnp.bfloat16)
        home(1, True)

    def whole(slot):
        for i in range(2):
            done = accum[0, slot // 2, i]
            result[slot, i] = (done[:, :HD] / done[:, HD:]).astype(jnp.bfloat16)
        home(slot, True)

    def results_in(h):
        for m in range(2):
            for f in range(2):
                arrive(merged.at[h, m, :, lanes(2 * f + core)], o_sem.at[h, m, f])
                hand_over(h, m, f, True)

    def handed(h):
        for m in range(2):
            for f in range(2):
                arrive(merged.at[h, m, :, lanes(2 * f + 1 - core)], hand_sem.at[h, m, f])

    def term(h, m, columns):
        weight = (w_control, w_base)[m]
        rows = weight[:, lanes(h), columns].reshape(4 * HD, -1)
        return jnp.dot(merged[h, m], rows, preferred_element_type=jnp.float32)

    def project(h, first=False):
        handed(h)
        for m in range(2):
            new = term(h, m, slice(None))
            proj[m] = new if first else proj[m] + new

    pairs_out(0, True)
    pairs_out(1, True)
    queries_out(0, True)
    queries_out(2, True)
    queries_out(1, True)
    for copy in locals_in:
        copy.start()
    best[...] = jnp.full(best.shape, NEG, jnp.float32)
    accum[...] = jnp.zeros(accum.shape, jnp.float32)
    blocks_in(0)
    blocks_in(1)
    pairs_out(2, True)
    queries_in(1, 0)
    for i in range(2):
        query_across(i, True)
    queries_in(0, 0)
    queries_in(0, 1)

    steps = ((0, 0), (1, 0), (0, 1), (0, 2), (1, 1), (0, 3), (1, 2), (1, 3))

    def pick(t, which):
        found = jnp.int32(steps[0][which])
        for k, entry in enumerate(steps):
            found = jnp.where(t == k, entry[which], found)
        return found

    def step(t, carry):
        slot, block = pick(t, 0), pick(t, 1)

        @pl.when(t == 1)
        def _():
            weights_across(True)
            weights_beside(True)
            neighbours_in(0)
            queries_in(1, 1)

        @pl.when(t == 2)
        def _():
            blocks_in(2)

        @pl.when(t == 3)
        def _():
            neighbours_in(1)

        @pl.when(t == 4)
        def _():
            far_in(0)

        @pl.when(t == 5)
        def _():
            neighbours_in(2)
            far_in(1)
            for c in range(2):
                arrive(w_base.at[2 * (1 - half) + c, share], w_sem.at[1 + c])
            weights_along(True)

        @pl.when(t == 7)
        def _():
            far_in(2)

        relayed(slot, block)
        update([(p, i, slice(0, ROWS)) for p in range(2) for i in range(2)], slot, block, 1)
        return carry

    lax.fori_loop(0, len(steps), step, 0)
    part()
    for block in range(4):
        relayed(2, block)

    def last_step(t, carry):
        @pl.when(t == 2)
        def _():
            whole(2)
            combine()

        cut = ROWS // 2
        tiles = [(1 - t // 2, i, slice(k * cut, (k + 1) * cut)) for i in range(2) for k in range(2)]
        update(tiles, 2, 2 * (t % 2), 2)
        return carry

    lax.fori_loop(0, 4, last_step, 0)
    whole(0)

    for h in range(3):
        pairs_out(h, False)
        queries_out(h, False)
        for i in range(2):
            ring_out(h, i, False)
            keys_on(h, i, False)
            values_on(h, i, False)
            far_on(h, i, False)
    for i in range(2):
        query_across(i, False)
    part_across(False)
    weights_beside(False)
    weights_across(False)
    weights_along(False)
    for copy in locals_in:
        copy.wait()
    arrive(w_base.at[2 * half + 1 - core], w_sem.at[0])
    for d in range(1, 4):
        rows = pl.ds(pl.multiple_of(SHARE * ((x + 4 - d) % 4), SHARE), SHARE)
        arrive(w_base.at[pl.ds(2 * (1 - half), 2), rows], w_sem.at[2 + d])
    results_in(1)
    project(1, True)
    results_in(2 * (1 - y))
    project(2 * (1 - y))
    results_in(2 * y)
    handed(2 * y)
    per_row = WIDTH // HD
    for k in range(3):
        columns = slice(2 * k * HD, (2 * k + 2) * HD)
        gates = [
            jnp.concatenate([gate[pl.ds(grp * per_row + 2 * k + j, 1), :] for j in range(2)], axis=1)
            for gate in (control_gate, base_gate)
        ]
        sums = [proj[m, :, columns] + term(2 * y, m, columns) for m in range(2)]
        first = (x_control[:, columns].astype(jnp.float32) + gates[0] * sums[0]).astype(jnp.bfloat16)
        outs[0, :, columns] = first
        second = x_base[:, columns].astype(jnp.float32) + gates[1] * sums[1]
        outs[1, :, columns] = (second + first.astype(jnp.float32)).astype(jnp.bfloat16)

    for h in range(3):
        home(h, False)
        for m in range(2):
            for f in range(2):
                hand_over(h, m, f, False)


def on_device(
    control_x, control_qkv, control_out_w, control_gate, base_x, base_qkv, base_out_w, base_gate
):
    vmem = pl.BlockSpec(memory_space=pltpu.VMEM)
    anywhere = pl.BlockSpec(memory_space=pl.ANY)
    dma = pltpu.SemaphoreType.DMA
    half16 = jnp.bfloat16
    full32 = jnp.float32
    outs = pl.pallas_call(
        sublayer_kernel,
        out_shape=jax.ShapeDtypeStruct((2, ROWS, WIDTH), half16),
        in_specs=[anywhere, anywhere, anywhere, vmem, anywhere, anywhere, anywhere, vmem],
        out_specs=vmem,
        scratch_shapes=[
            pltpu.VMEM((3, 2, 4, 2, 2, ROWS, HD), half16),
            pltpu.VMEM((2, 2, 2, ROWS, HD), half16),
            pltpu.VMEM((2, 2, 2, ROWS, HD), full32),
            pltpu.VMEM((2, 2, 2, ROWS, 2 * HD), full32),
            pltpu.VMEM((3, ROWS, HD), half16),
            pltpu.VMEM((3, ROWS, HD), half16),
            pltpu.VMEM((3, 2, ROWS, HD), half16),
            pltpu.VMEM((3, 2, ROWS, 4 * HD), half16),
            pltpu.VMEM((4, GROUP, WIDTH), half16),
            pltpu.VMEM((4, GROUP, WIDTH), half16),
            pltpu.VMEM((2, ROWS, WIDTH), full32),
            pltpu.VMEM((ROWS, WIDTH), half16),
            pltpu.VMEM((ROWS, WIDTH), half16),
            dma((3, 2)),
            dma((2, 2, 2)),
            dma((3, 2, 2)),
            dma((3, 2, 2)),
            dma((3, 4, 2)),
            dma((1,)),
            dma((3, 2, 2)),
            dma((3, 2, 2)),
            dma((6,)),
            dma((4,)),
            dma((3 * PER_HEAD + 6,)),
        ],
        compiler_params=pltpu.CompilerParams(
            collective_id=0, has_side_effects=True, vmem_limit_bytes=60 * 2**20
        ),
        name="sublayer",
    )(
        control_x,
        control_qkv.transpose(1, 0, 2),
        control_out_w.reshape(4, GROUP, 4 * WIDTH),
        control_gate.reshape(4 * WIDTH // HD, HD),
        base_x,
        base_qkv.transpose(1, 0, 2),
        base_out_w,
        base_gate.reshape(4 * WIDTH // HD, HD),
    )
    return outs[0], outs[1]


def solution(mesh):
    in_specs = (
        P("seq", None),
        P("seq", None, None),
        P(),
        P(),
        P("seq", "grp"),
        P("seq", None, "grp"),
        P("grp", None),
        P(),
    )
    out_specs = (P("seq", "grp"), P("seq", "grp"))
    return jax.shard_map(
        on_device, mesh=mesh, in_specs=in_specs, out_specs=out_specs, check_vma=False
    )
```

```python
import math

import jax
import jax.numpy as jnp
from jax import lax
from jax.experimental import pallas as pl
from jax.experimental.pallas import tpu as pltpu
from jax.sharding import PartitionSpec as P

HD = 128
ROWS = 320
WIDTH = 768
GROUP = 3 * HD
SHARE = GROUP // 4
SCALE = 1.4426950408889634 / math.sqrt(HD)
NEG = -1e30
NT = (((1,), (1,)), ((), ()))
PER_HEAD = 31


def sublayer_kernel(
    control_x,
    control,
    control_w,
    control_gate,
    base_x,
    base,
    base_w,
    base_gate,
    outs,
    kv,
    queries,
    best,
    accum,
    part_out,
    part_in,
    result,
    merged,
    w_control,
    w_base,
    proj,
    x_control,
    x_base,
    x_sem,
    q_sem,
    z_sem,
    far_sem,
    relay_sem,
    part_sem,
    o_sem,
    hand_sem,
    w_sem,
    local_sem,
    send_sem,
):
    grp = lax.axis_index("grp")
    seq = lax.axis_index("seq")
    half, core, y, z, x = grp // 2, grp % 2, seq // 16, (seq // 4) % 4, seq % 4
    here = (half, core, y, z, x)
    sibling = (half, 1 - core, y, z, x)
    above = (half, core, y, (z + 1) % 4, x)
    below = (half, core, y, (z + 3) % 4, x)
    right = (half, core, y, z, (x + 1) % 4)
    left = (half, core, y, z, (x + 3) % 4)
    across = (half, core, 1 - y, z, x)

    def ident(device):
        return {"grp": 2 * device[0] + device[1], "seq": 16 * device[2] + 4 * device[3] + device[4]}

    barrier = pltpu.get_barrier_semaphore()
    greeted = (
        [sibling, above, below, right, left, across]
        + [(half, core, y, z, (x + 2) % 4), (half, core, y, (z + 2) % 4, x)]
        + [(half, x % 2, p, z, 2 * core + i) for i in range(2) for p in (y, 1 - y)]
        + [(half, z % 2, y, 2 * core + i, x) for i in range(2)]
        + [(f, x // 2, p, z, 2 * m + core) for f in range(2) for m in range(2) for p in (y, 1 - y)]
        + [(f, z // 2, y, 2 * m + core, x) for f in range(2) for m in range(2)]
        + [(1 - half, i, y, z, x) for i in range(2)]
    )
    for device in greeted:
        pl.semaphore_signal(barrier, inc=1, device_id=ident(device))

    lanes_out = pl.ds(pl.multiple_of(grp * WIDTH, WIDTH), WIDTH)
    locals_in = [
        pltpu.make_async_copy(control_w.at[:, :, lanes_out], w_control, local_sem.at[0]),
        pltpu.make_async_copy(base_w.at[:, lanes_out], w_base.at[grp], local_sem.at[1]),
        pltpu.make_async_copy(control_x.at[:, lanes_out], x_control, local_sem.at[2]),
        pltpu.make_async_copy(base_x, x_base, local_sem.at[3]),
    ]

    pl.semaphore_wait(barrier, len(greeted))

    def send(number, source, target, arrived, device, start, may_be_here=False):
        remote = pltpu.make_async_remote_copy(
            source, target, send_sem.at[number], arrived, device_id=ident(device)
        )
        act = remote.start if start else remote.wait_send
        if not may_be_here:
            act()
            return
        own = device[0] == here[0]
        for left, right in zip(device[1:], here[1:]):
            own = jnp.logical_and(own, left == right)
        pl.when(jnp.logical_not(own))(act)
        if start:

            @pl.when(own)
            def _():
                pltpu.make_async_copy(source, target, arrived).start()

    def arrive(ref, sem):
        pltpu.make_async_copy(ref, ref, sem).wait()

    def lanes(index):
        return pl.ds(pl.multiple_of(index * HD, HD), HD)

    def route(slot, m):
        if slot == 1:
            return 1, z % 2, (half, z // 2, y, 2 * m + core, x)
        plane = y if slot == 0 else 1 - y
        return 2 * plane, x % 2, (half, x // 2, plane, z, 2 * m + core)

    def pairs_out(slot, start):
        for m, ref, first in ((0, control, 3 * grp), (1, base, 0)):
            head, i, device = route(slot, m)
            send(
                PER_HEAD * slot + m,
                ref.at[pl.ds(1, 2), :, lanes(first + head)],
                kv.at[slot, :, 0, 0, i],
                x_sem.at[slot, i],
                device,
                start,
                True,
            )

    def queries_out(slot, start):
        for m, ref, first in ((0, control, 3 * grp), (1, base, 0)):
            head, i, device = route(slot, m)
            send(
                PER_HEAD * slot + 2 + m,
                ref.at[0, :, lanes(first + head)],
                queries.at[slot % 2, slot // 2, i],
                q_sem.at[slot % 2, slot // 2, i],
                device,
                start,
                True,
            )

    def ahead(h):
        return right if h == 1 else above

    def behind(h):
        return left if h == 1 else below

    def ring_out(h, i, start):
        block = kv.at[h, :, 0, 0, i]
        number = PER_HEAD * h + i
        send(number + 4, block, kv.at[h, :, 1, 0, i], z_sem.at[h, 0, i], ahead(h), start)
        send(number + 6, block, kv.at[h, :, 2, 0, i], z_sem.at[h, 1, i], behind(h), start)
        send(number + 8, block, kv.at[h, :, 0, 1, i], relay_sem.at[h, 0, i], sibling, start)

    def query_across(i, start):
        send(
            PER_HEAD + 10 + i,
            queries.at[1, 0, i],
            queries.at[1, 1, i],
            q_sem.at[1, 1, i],
            across,
            start,
        )

    def keys_on(h, i, start):
        number = PER_HEAD * h + i
        send(number + 12, kv.at[h, 0, 1, 0, i], kv.at[h, 0, 3, 0, i], far_sem.at[h, 0, i], ahead(h), start)
        block = kv.at[h, :, 1, 0, i]
        send(number + 16, block, kv.at[h, :, 1, 1, i], relay_sem.at[h, 1, i], sibling, start)

    def values_on(h, i, start):
        number = PER_HEAD * h + i
        send(number + 14, kv.at[h, 1, 2, 0, i], kv.at[h, 1, 3, 0, i], far_sem.at[h, 1, i], behind(h), start)
        block = kv.at[h, :, 2, 0, i]
        send(number + 18, block, kv.at[h, :, 2, 1, i], relay_sem.at[h, 2, i], sibling, start)

    def far_on(h, i, start):
        block = kv.at[h, :, 3, 0, i]
        send(PER_HEAD * h + 20 + i, block, kv.at[h, :, 3, 1, i], relay_sem.at[h, 3, i], sibling, start)

    def part_across(start):
        send(PER_HEAD + 22, part_out, part_in, part_sem.at[0], across, start)

    def home(slot, start):
        head, place = (1, z) if slot == 1 else (2 * y, x)
        for i in range(2):
            for f in range(2):
                if slot == 1:
                    owner = (f, z % 2, y, 2 * core + i, x)
                else:
                    owner = (f, x % 2, y if slot == 0 else 1 - y, z, 2 * core + i)
                send(
                    PER_HEAD * slot + 23 + 2 * i + f,
                    result.at[slot, i],
                    merged.at[head, place // 2, :, lanes(2 * half + place % 2)],
                    o_sem.at[head, place // 2, half],
                    owner,
                    start,
                    True,
                )

    def hand_over(h, m, f, start):
        block = merged.at[h, m, :, lanes(2 * f + core)]
        send(PER_HEAD * h + 27 + 2 * m + f, block, block, hand_sem.at[h, m, f], sibling, start)

    last = 3 * PER_HEAD
    def share(place):
        return pl.ds(pl.multiple_of(SHARE * place, SHARE), SHARE)

    def weights_beside(start):
        columns = pl.ds(pl.multiple_of((2 * half + 1 - core) * WIDTH, WIDTH), WIDTH)
        send(last, base_w.at[:, columns], w_base.at[grp], w_sem.at[0], sibling, start)

    def weights_across(start):
        rows = share(jnp.where(core == 0, x, z))
        for c in range(2):
            columns = pl.ds(pl.multiple_of((2 * (1 - half) + c) * WIDTH, WIDTH), WIDTH)
            send(
                last + 1 + c,
                base_w.at[rows, columns],
                w_base.at[grp, rows],
                w_sem.at[1 + core],
                (1 - half, c, y, z, x),
                start,
            )

    def weights_along(start):
        for d in range(1, 4):
            block = w_base.at[2 * (1 - half), share(x)]
            device = (half, core, y, z, (x + d) % 4)
            send(last + 2 + d, block, block, w_sem.at[2 + d], device, start)
            block = w_base.at[2 * (1 - half) + 1, share(z)]
            device = (half, core, y, (z + d) % 4, x)
            send(last + 5 + d, block, block, w_sem.at[5 + d], device, start)

    def order(h):
        place = z if h == 1 else x
        near = jnp.where(place // 2 == core, place % 2, 1 - place % 2)
        return near, 1 - near

    def blocks_in(h):
        for i in order(h):
            arrive(kv.at[h, :, 0, 0, i], x_sem.at[h, i])
            ring_out(h, i, True)

    def queries_in(group, side):
        for i in range(2):
            arrive(queries.at[group, side, i], q_sem.at[group, side, i])

    def neighbours_in(h):
        for i in order(h):
            arrive(kv.at[h, :, 1, 0, i], z_sem.at[h, 0, i])
            keys_on(h, i, True)
            arrive(kv.at[h, :, 2, 0, i], z_sem.at[h, 1, i])
            values_on(h, i, True)

    def far_in(h):
        for i in order(h):
            for j in range(2):
                arrive(kv.at[h, j, 3, 0, i], far_sem.at[h, j, i])
            far_on(h, i, True)

    def relayed(h, block):
        for i in range(2):
            arrive(kv.at[h, :, block, 1, i], relay_sem.at[h, block, i])

    def update(tiles, h, low, count):
        group = h % 2
        keys = kv[h, 0, pl.ds(low, count)].reshape(count * 4 * ROWS, HD)
        values = kv[h, 1, pl.ds(low, count)].reshape(count * 4 * ROWS, HD)
        values = jnp.concatenate([values, jnp.ones_like(values)], axis=1)
        for p, i, rows in tiles:
            scores = lax.dot_general(
                queries[group, p, i, rows], keys, NT, preferred_element_type=jnp.float32
            )
            old = best[group, p, i, rows][:, :1]
            new = jnp.maximum(old, jnp.max(scores, axis=1, keepdims=True))
            weights = jnp.exp2(scores * SCALE - new * SCALE).astype(jnp.bfloat16)
            keep = jnp.exp2((old - new) * SCALE)
            best[group, p, i, rows] = jnp.broadcast_to(new, (new.shape[0], HD))
            accum[group, p, i, rows] = accum[group, p, i, rows] * keep + jnp.dot(
                weights, values, preferred_element_type=jnp.float32
            )

    lane = lax.broadcasted_iota(jnp.int32, (ROWS, HD), 1)

    def outcome(side, i):
        total = accum[1, side, i][:, HD:]
        return accum[1, side, i][:, :HD] / total, best[1, side, i] * SCALE + jnp.log2(total)

    def part():
        packed = jnp.zeros((ROWS, HD), jnp.float32)
        for i in range(2):
            value, rest = outcome(1, i)
            part_out[i] = value.astype(jnp.bfloat16)
            for j in range(3):
                piece = rest.astype(jnp.bfloat16).astype(jnp.float32)
                packed = jnp.where(lane == 3 * i + j, piece, packed)
                rest = rest - piece
        part_out[2] = packed.astype(jnp.bfloat16)
        part_across(True)

    def combine():
        arrive(part_in, part_sem.at[0])
        packed = part_in[2].astype(jnp.float32)
        for i in range(2):
            value, log_sum = outcome(0, i)
            other = (
                packed[:, 3 * i : 3 * i + 1]
                + packed[:, 3 * i + 1 : 3 * i + 2]
                + packed[:, 3 * i + 2 : 3 * i + 3]
            )
            top = jnp.maximum(log_sum, other)
            mine = jnp.exp2(log_sum - top)
            theirs = jnp.exp2(other - top)
            mixed = value * mine + part_in[i].astype(jnp.float32) * theirs
            result[1, i] = (mixed / (mine + theirs)).astype(jnp.bfloat16)
        home(1, True)

    def whole(slot):
        for i in range(2):
            done = accum[0, slot // 2, i]
            result[slot, i] = (done[:, :HD] / done[:, HD:]).astype(jnp.bfloat16)
        home(slot, True)

    def results_in(h):
        for m in range(2):
            for f in range(2):
                arrive(merged.at[h, m, :, lanes(2 * f + core)], o_sem.at[h, m, f])
                hand_over(h, m, f, True)

    def handed(h):
        for m in range(2):
            for f in range(2):
                arrive(merged.at[h, m, :, lanes(2 * f + 1 - core)], hand_sem.at[h, m, f])

    def term(h, m, columns):
        weight = (w_control, w_base)[m]
        rows = weight[:, lanes(h), columns].reshape(4 * HD, -1)
        return jnp.dot(merged[h, m], rows, preferred_element_type=jnp.float32)

    def project(h, first=False):
        handed(h)
        for m in range(2):
            new = term(h, m, slice(None))
            proj[m] = new if first else proj[m] + new

    pairs_out(0, True)
    pairs_out(1, True)
    queries_out(0, True)
    queries_out(2, True)
    queries_out(1, True)
    for copy in locals_in:
        copy.start()
    best[...] = jnp.full(best.shape, NEG, jnp.float32)
    accum[...] = jnp.zeros(accum.shape, jnp.float32)
    blocks_in(0)
    blocks_in(1)
    pairs_out(2, True)
    queries_in(1, 0)
    for i in range(2):
        query_across(i, True)
    queries_in(0, 0)
    queries_in(0, 1)

    steps = ((0, 0), (1, 0), (0, 1), (0, 2), (1, 1), (0, 3), (1, 2), (1, 3))

    def pick(t, which):
        found = jnp.int32(steps[0][which])
        for k, entry in enumerate(steps):
            found = jnp.where(t == k, entry[which], found)
        return found

    def step(t, carry):
        slot, block = pick(t, 0), pick(t, 1)

        @pl.when(t == 1)
        def _():
            weights_across(True)
            weights_beside(True)
            neighbours_in(0)
            queries_in(1, 1)

        @pl.when(t == 2)
        def _():
            blocks_in(2)

        @pl.when(t == 3)
        def _():
            neighbours_in(1)

        @pl.when(t == 4)
        def _():
            far_in(0)

        @pl.when(t == 5)
        def _():
            neighbours_in(2)
            far_in(1)
            for c in range(2):
                arrive(w_base.at[2 * (1 - half) + c, share((x, z)[c])], w_sem.at[1 + c])
            weights_along(True)

        @pl.when(t == 7)
        def _():
            far_in(2)

        relayed(slot, block)
        update([(p, i, slice(0, ROWS)) for p in range(2) for i in range(2)], slot, block, 1)
        return carry

    lax.fori_loop(0, len(steps), step, 0)
    part()
    for block in range(4):
        relayed(2, block)

    def last_step(t, carry):
        @pl.when(t == 2)
        def _():
            whole(2)
            combine()

        cut = ROWS // 2
        tiles = [(1 - t // 2, i, slice(k * cut, (k + 1) * cut)) for i in range(2) for k in range(2)]
        update(tiles, 2, 2 * (t % 2), 2)
        return carry

    lax.fori_loop(0, 4, last_step, 0)
    whole(0)

    for h in range(3):
        pairs_out(h, False)
        queries_out(h, False)
        for i in range(2):
            ring_out(h, i, False)
            keys_on(h, i, False)
            values_on(h, i, False)
            far_on(h, i, False)
    for i in range(2):
        query_across(i, False)
    part_across(False)
    weights_beside(False)
    weights_across(False)
    weights_along(False)
    for copy in locals_in:
        copy.wait()
    arrive(w_base.at[2 * half + 1 - core], w_sem.at[0])
    for d in range(1, 4):
        arrive(w_base.at[2 * (1 - half), share((x + 4 - d) % 4)], w_sem.at[2 + d])
        arrive(w_base.at[2 * (1 - half) + 1, share((z + 4 - d) % 4)], w_sem.at[5 + d])
    results_in(1)
    project(1, True)
    results_in(2 * (1 - y))
    project(2 * (1 - y))
    results_in(2 * y)
    handed(2 * y)
    per_row = WIDTH // HD
    for k in range(3):
        columns = slice(2 * k * HD, (2 * k + 2) * HD)
        gates = [
            jnp.concatenate([gate[pl.ds(grp * per_row + 2 * k + j, 1), :] for j in range(2)], axis=1)
            for gate in (control_gate, base_gate)
        ]
        sums = [proj[m, :, columns] + term(2 * y, m, columns) for m in range(2)]
        first = (x_control[:, columns].astype(jnp.float32) + gates[0] * sums[0]).astype(jnp.bfloat16)
        outs[0, :, columns] = first
        second = x_base[:, columns].astype(jnp.float32) + gates[1] * sums[1]
        outs[1, :, columns] = (second + first.astype(jnp.float32)).astype(jnp.bfloat16)

    for h in range(3):
        home(h, False)
        for m in range(2):
            for f in range(2):
                hand_over(h, m, f, False)


def on_device(
    control_x, control_qkv, control_out_w, control_gate, base_x, base_qkv, base_out_w, base_gate
):
    vmem = pl.BlockSpec(memory_space=pltpu.VMEM)
    anywhere = pl.BlockSpec(memory_space=pl.ANY)
    dma = pltpu.SemaphoreType.DMA
    half16 = jnp.bfloat16
    full32 = jnp.float32
    outs = pl.pallas_call(
        sublayer_kernel,
        out_shape=jax.ShapeDtypeStruct((2, ROWS, WIDTH), half16),
        in_specs=[anywhere, anywhere, anywhere, vmem, anywhere, anywhere, anywhere, vmem],
        out_specs=vmem,
        scratch_shapes=[
            pltpu.VMEM((3, 2, 4, 2, 2, ROWS, HD), half16),
            pltpu.VMEM((2, 2, 2, ROWS, HD), half16),
            pltpu.VMEM((2, 2, 2, ROWS, HD), full32),
            pltpu.VMEM((2, 2, 2, ROWS, 2 * HD), full32),
            pltpu.VMEM((3, ROWS, HD), half16),
            pltpu.VMEM((3, ROWS, HD), half16),
            pltpu.VMEM((3, 2, ROWS, HD), half16),
            pltpu.VMEM((3, 2, ROWS, 4 * HD), half16),
            pltpu.VMEM((4, GROUP, WIDTH), half16),
            pltpu.VMEM((4, GROUP, WIDTH), half16),
            pltpu.VMEM((2, ROWS, WIDTH), full32),
            pltpu.VMEM((ROWS, WIDTH), half16),
            pltpu.VMEM((ROWS, WIDTH), half16),
            dma((3, 2)),
            dma((2, 2, 2)),
            dma((3, 2, 2)),
            dma((3, 2, 2)),
            dma((3, 4, 2)),
            dma((1,)),
            dma((3, 2, 2)),
            dma((3, 2, 2)),
            dma((9,)),
            dma((4,)),
            dma((3 * PER_HEAD + 9,)),
        ],
        compiler_params=pltpu.CompilerParams(
            collective_id=0, has_side_effects=True, vmem_limit_bytes=60 * 2**20
        ),
        name="sublayer",
    )(
        control_x,
        control_qkv.transpose(1, 0, 2),
        control_out_w.reshape(4, GROUP, 4 * WIDTH),
        control_gate.reshape(4 * WIDTH // HD, HD),
        base_x,
        base_qkv.transpose(1, 0, 2),
        base_out_w,
        base_gate.reshape(4 * WIDTH // HD, HD),
    )
    return outs[0], outs[1]


def solution(mesh):
    in_specs = (
        P("seq", None),
        P("seq", None, None),
        P(),
        P(),
        P("seq", "grp"),
        P("seq", None, "grp"),
        P("grp", None),
        P(),
    )
    out_specs = (P("seq", "grp"), P("seq", "grp"))
    return jax.shard_map(
        on_device, mesh=mesh, in_specs=in_specs, out_specs=out_specs, check_vma=False
    )
```
